256 devices in a mesh: dz: 4 (over z_lo, core), dxy: 64 (over z_hi, y, x).
Axes of the slice: x: 4, y: 4, z: 8 (z_hi: 4, z_lo: 2; z = z_hi * 2 + z_lo), core: 2. Of those that a mesh axis runs over, the one named last changes fastest.
Arguments:
- queries: bfloat16 [32768, 1024], P(('dz', 'dxy')), may hold values from -180 to 180
- keys: bfloat16 [32768, 1024], P(('dz', 'dxy')), may hold values from -4 to 4
- values: bfloat16 [32768, 1024], P(('dz', 'dxy')), may hold values from -6 to 6
- out_grad: bfloat16 [32768, 1024], P(('dz', 'dxy')), may hold values from -24 to 24
- out_weight: bfloat16 [1024, 1024], replicated, may hold values from -0.1875 to 0.1875
- pair_counts: int32 [256, 9], P(('dz', 'dxy')), may hold values from 0 to 128, as said below
- counts: int32 [256], P(('dz', 'dxy')), may hold values from 2 to 128
Outputs:
- gradient_of_queries: bfloat16 [32768, 1024], P(('dz', 'dxy'))
- gradient_of_keys: bfloat16 [32768, 1024], P(('dz', 'dxy'))
- gradient_of_values: bfloat16 [32768, 1024], P(('dz', 'dxy'))
- wo_grad: float32 [1024, 1024], P('dxy')
The draws below stay inside these ranges and needn't reach their ends.
Inputs may be any that keep to these rules, and one draw needn't show every extreme that they name: `pair_counts`: slot ((i + 1) * 3 + (j + 1)) + t of cell c refers to cell t of the domain at offset (i, j) from c's domain; its entry is that cell's entry of counts when the two cells are linked, else 0, and always 0 where the domain lies outside the grid. Links are symmetric and every cell is linked to itself.
All inputs are finite; a program needn't handle non-finite values.
Results may differ from the reference program's by a relative error of at most 0.02.
Values may be sent and summed in bfloat16 or wider, within the bound.
A program may use at most 128 MiB of HBM per device.

```python
import jax
import jax.numpy as jnp
from jax import lax

D = 1024
HEADS = 16
HEAD_DIM = 64
CELL = 128
CPD = 1
NB = 9
CELLS = 256
ATOMS = 32768
N_DZ = 4
N_DXY = 64


def cell_tables(key):
    base_key = jax.random.fold_in(key, 11)
    key_raw, key_pore, key_link = jax.random.split(base_key, 3)
    cell_total = CPD * N_DZ * N_DXY
    cell_ids = jnp.arange(cell_total, dtype=jnp.int32)
    raw_fill = jax.random.randint(key_raw, (cell_total,), 0, CELL - 1)
    layer_index = cell_ids // CPD // N_DXY
    factor = jnp.where(layer_index == N_DZ - 1, 1, 8)
    pore_mask = jax.random.randint(key_pore, (cell_total,), 0, 8) == 0
    factor = jnp.where(pore_mask, 1, factor)
    filled = 2 + raw_fill * factor // 8
    filled = filled.at[0].set(CELL).astype(jnp.int32)
    colour = jax.random.randint(key_link, (cell_total,), 0, 3)
    slot_ids = jnp.arange(9 * CPD, dtype=jnp.int32)
    offset_z = slot_ids // (3 * CPD) - 1
    offset_xy = slot_ids // CPD % 3 - 1
    local_cell = slot_ids % CPD
    domain = cell_ids // CPD
    layer_z = domain[:, None] // N_DXY + offset_z[None, :]
    place_xy = domain[:, None] % N_DXY + offset_xy[None, :]
    inside = (layer_z >= 0) & (layer_z < N_DZ) & (place_xy >= 0) & (place_xy < N_DXY)
    neighbour = (jnp.clip(layer_z, 0, N_DZ - 1) * N_DXY + jnp.clip(place_xy, 0, N_DXY - 1)) * CPD + local_cell[None, :]
    linked = (neighbour == cell_ids[:, None]) | ((colour[:, None] + colour[neighbour]) % 3 != 0)
    pair_table = jnp.where(inside & linked, filled[neighbour], 0).astype(jnp.int32)
    return (filled, pair_table)


def draw_counts(key, part):
    return cell_tables(key)[0]


def draw_pair_counts(key, part):
    return cell_tables(key)[1]


def query_key_pair(key):
    base_key = jax.random.fold_in(key, 23)
    key_first, key_second = jax.random.split(base_key)
    atom_total = CELL * CPD * N_DZ * N_DXY
    key_rows = jnp.clip(jax.random.normal(key_first, (atom_total, D), jnp.float32), -4.0, 4.0)
    query_rows = 2.0 * jnp.clip(jax.random.normal(key_second, (atom_total, D), jnp.float32), -4.0, 4.0)
    return (query_rows, key_rows)


def draw_queries(key, part):
    return query_key_pair(key)[0].astype(jnp.bfloat16)


def draw_keys(key, part):
    return query_key_pair(key)[1].astype(jnp.bfloat16)


def strengthened(values, stream_key, source, target, blocks, factor):
    owner, partner = [(jnp.arange(values.shape[axis_at]) // (values.shape[axis_at] // blocks)).reshape([-1 if axis == axis_at else 1 for axis in range(values.ndim)]) for axis_at in (source, target)]
    chosen = jax.random.permutation(stream_key, blocks)[partner]
    strong = (owner == chosen) | (owner == (partner + blocks // 2) % blocks)
    return jnp.where(strong, factor * values, values)


def level_of(stream_key, shape, shards, low, largest):
    factor_of = 1.0
    for dim, shards_of in shards:
        steps = jax.random.uniform(jax.random.fold_in(jax.random.fold_in(stream_key, 6), dim), (shards_of,), jnp.float32, low / len(shards), largest / len(shards))
        factor_of = factor_of * jnp.repeat(jnp.exp(steps), shape[dim] // shards_of).reshape((-1,) + (1,) * (len(shape) - 1 - dim))
    return factor_of


def normal_values(stream_key, shape, scale, most, pieces=(), held_as=jnp.bfloat16):
    loudness = level_of(stream_key, shape, pieces, -0.22, 0.18) if pieces else 1.0
    array = jax.random.normal(stream_key, shape, jnp.float32) * scale * loudness
    return jnp.minimum(jnp.maximum(array, -most), most).astype(held_as)


def bell_draw_with(key, extent, scale, most, cuts, heavy, kind=jnp.bfloat16):
    array = scale * jax.random.normal(key, extent, jnp.float32)
    if cuts:
        array = array * level_of(key, extent, cuts, -0.22, 0.18)
    return jnp.clip(strengthened(array, jax.random.fold_in(key, 3), *heavy), -most, most).astype(kind)


def setup_inputs(seed: int = 0) -> dict:
    key_of = jax.random.split(jax.random.key(seed), 8)
    return {
        "queries": draw_queries(jax.random.fold_in(key_of[7], 71), 0),
        "keys": draw_keys(jax.random.fold_in(key_of[7], 71), 0),
        "values": normal_values(key_of[2], (ATOMS, D), 1.0, 6.0, ((0, 256),)),
        "out_grad": bell_draw_with(key_of[3], (ATOMS, D), 1.0, 24.0, ((0, 256),), (0, 1, 256, 6.0)),
        "out_weight": normal_values(key_of[4], (D, D), D ** -0.5, 0.1875),
        "pair_counts": draw_pair_counts(jax.random.fold_in(key_of[7], 71), 0),
        "counts": draw_counts(jax.random.fold_in(key_of[7], 71), 0),
    }


def neighbour_cells(cell_ids):
    slot_ids = jnp.arange(NB, dtype=jnp.int32)
    offset_z = slot_ids // (3 * CPD) - 1
    offset_xy = (slot_ids // CPD) % 3 - 1
    local_cell = slot_ids % CPD
    domain = cell_ids // CPD
    layer_z = domain[:, None] // N_DXY + offset_z[None, :]
    place_xy = domain[:, None] % N_DXY + offset_xy[None, :]
    inside = (layer_z >= 0) & (layer_z < N_DZ) & (place_xy >= 0) & (place_xy < N_DXY)
    target = (jnp.clip(layer_z, 0, N_DZ - 1) * N_DXY + jnp.clip(place_xy, 0, N_DXY - 1)) * CPD + local_cell[None, :]
    return target.astype(jnp.int32), inside


def reference(queries, keys, values, out_grad, out_weight, pair_counts, counts):
    logit_scale = HEAD_DIM ** -0.5
    atom_index = jnp.arange(CELL, dtype=jnp.int32)
    live_rows = (atom_index[None, :] < counts[:, None]).reshape(ATOMS, 1)
    masked_grad = jnp.where(live_rows, out_grad, jnp.zeros_like(out_grad))
    out_delta = jnp.dot(masked_grad, out_weight, preferred_element_type=jnp.float32).astype(jnp.bfloat16)
    cell_shape = (CELLS, CELL, HEADS, HEAD_DIM)
    query_cells = queries.reshape(cell_shape)
    key_cells = keys.reshape(cell_shape)
    value_cells = values.reshape(cell_shape)
    delta_cells = out_delta.reshape(cell_shape)
    cell_ids = jnp.arange(CELLS, dtype=jnp.int32)
    target, inside = neighbour_cells(cell_ids)

    def query_side(cell_id):
        near_cells = target[cell_id]
        adjacent_keys = key_cells[near_cells].reshape(NB * CELL, HEADS, HEAD_DIM).astype(jnp.float32)
        adjacent_values = value_cells[near_cells].reshape(NB * CELL, HEADS, HEAD_DIM).astype(jnp.float32)
        allowed = (atom_index[None, :] < pair_counts[cell_id][:, None]).reshape(NB * CELL)
        home_cell_queries = query_cells[cell_id].astype(jnp.float32)
        home_cell_delta = delta_cells[cell_id].astype(jnp.float32)
        attention_logits = logit_scale * jnp.einsum("qvy,pvy->vqp", home_cell_queries, adjacent_keys)
        attention_logits = jnp.where(allowed[None, None, :], attention_logits, -1e30)
        highest = jnp.max(attention_logits, axis=-1, keepdims=True)
        weight_sum = jnp.sum(jnp.where(allowed[None, None, :], jnp.exp(attention_logits - highest), 0.0), axis=-1, keepdims=True)
        log_total = highest + jnp.log(weight_sum)
        probs = jnp.where(allowed[None, None, :], jnp.exp(attention_logits - log_total), 0.0)
        probabilities_reduced = probs.astype(jnp.bfloat16)
        attention_result = jnp.einsum("gtl,lgs->tgs", probabilities_reduced.astype(jnp.float32), adjacent_values).astype(jnp.bfloat16)
        row_delta = jnp.sum(home_cell_delta * attention_result.astype(jnp.float32), axis=-1)
        probability_gradient = jnp.einsum("qvy,pvy->vqp", home_cell_delta, adjacent_values)
        score_gradient = (probs * (probability_gradient - row_delta.T[:, :, None])).astype(jnp.bfloat16)
        gradient_of_queries = (logit_scale * jnp.einsum("gtl,lgs->tgs", score_gradient.astype(jnp.float32), adjacent_keys)).astype(jnp.bfloat16)
        return gradient_of_queries.reshape(CELL, D), attention_result.reshape(CELL, D), log_total[:, :, 0], row_delta.T

    query_grads, attended_cells, log_totals, row_deltas = lax.map(query_side, cell_ids)

    def key_side(cell_id):
        near_cells = target[cell_id]
        near_inside = inside[cell_id]
        reverse_slot = ((8 - jnp.arange(NB, dtype=jnp.int32) // CPD) * CPD + cell_id % CPD).astype(jnp.int32)
        limit = jnp.where(near_inside, pair_counts[near_cells, reverse_slot], 0)
        allowed = jnp.broadcast_to(atom_index[None, None, :] < limit[:, None, None], (NB, CELL, CELL)).reshape(NB * CELL, CELL)
        adjacent_queries = query_cells[near_cells].reshape(NB * CELL, HEADS, HEAD_DIM).astype(jnp.float32)
        adjacent_delta = delta_cells[near_cells].reshape(NB * CELL, HEADS, HEAD_DIM).astype(jnp.float32)
        near_lse = jnp.transpose(log_totals[near_cells], (1, 0, 2)).reshape(HEADS, NB * CELL)
        near_rows = jnp.transpose(row_deltas[near_cells], (1, 0, 2)).reshape(HEADS, NB * CELL)
        home_cell_keys = key_cells[cell_id].astype(jnp.float32)
        home_cell_values = value_cells[cell_id].astype(jnp.float32)
        attention_logits = logit_scale * jnp.einsum("sfc,nfc->fsn", adjacent_queries, home_cell_keys)
        probs = jnp.where(allowed[None], jnp.exp(jnp.where(allowed[None], attention_logits - near_lse[:, :, None], 0.0)), 0.0)
        probabilities_reduced = probs.astype(jnp.bfloat16)
        probability_gradient = jnp.einsum("sfc,nfc->fsn", adjacent_delta, home_cell_values)
        score_gradient = (probs * (probability_gradient - near_rows[:, :, None])).astype(jnp.bfloat16)
        gradient_of_values = jnp.einsum("ucy,cuo->yuo", probabilities_reduced.astype(jnp.float32), adjacent_delta)
        gradient_of_keys = logit_scale * jnp.einsum("ucy,cuo->yuo", score_gradient.astype(jnp.float32), adjacent_queries)
        return gradient_of_keys.reshape(CELL, D).astype(jnp.bfloat16), gradient_of_values.reshape(CELL, D).astype(jnp.bfloat16)

    key_grads, value_grads = lax.map(key_side, cell_ids)
    attended_all = attended_cells.reshape(ATOMS, D)
    wo_grad = lax.dot_general(masked_grad, attended_all, (((0,), (0,)), ((), ())), preferred_element_type=jnp.float32) * ATOMS ** -0.5
    return query_grads.reshape(ATOMS, D), key_grads.reshape(ATOMS, D), value_grads.reshape(ATOMS, D), wo_grad
```

```python
import jax
import jax.numpy as jnp
from jax import lax
from jax.experimental import pallas as pl
from jax.experimental.pallas import tpu as pltpu
from jax.sharding import PartitionSpec as P

MESH = pl.DeviceIdType.MESH
BF = jnp.bfloat16
F32 = jnp.float32
CELL = 128
GW = 256
DOWN, UP = 0, 1
K_, V_, Q_, G_, C_ = 0, 1, 2, 3, 4
NEG = -1e30


def dot(a, b):
    return jnp.dot(a, b, preferred_element_type=F32)


def halves_t(x):
    row = lax.broadcasted_iota(jnp.int32, x.shape, 0)
    zero = jnp.zeros_like(x)
    return jnp.concatenate(
        [jnp.where(row < 64, x, zero), jnp.where(row < 64, zero, x)], axis=1
    )


def halves(x):
    lane = lax.broadcasted_iota(jnp.int32, x.shape, 1)
    zero = jnp.zeros_like(x)
    return jnp.concatenate(
        [jnp.where(lane < 64, x, zero), jnp.where(lane < 64, zero, x)], axis=0
    )


def diagonal(x):
    return jnp.concatenate([x[:64, :128], x[64:, 128:]], axis=0)


def kernel(
    q_hbm, k_hbm, v_hbm, g_hbm, w_hbm, pair_ref, count_ref,
    dq_hbm, dk_hbm, dv_hbm, wo_ref,
    kv, kvt, qs, gm, graw, gown, ww, do, pc, pcs,
    sbuf, pbuf, dsb, dos, delta, att, acc, dqs,
    hold, back, got, hold2, fin, wsum, wgot, x2, xgot,
    loc, a_s, a_r, b_s, b_r, l_s, l_r, d_s, d_r, m_s, m_r, f_s, f_r, u_s, u_r, x_s, x_r,
):
    me = lax.axis_index("dz")
    p = lax.axis_index("dxy")
    low = me < 2
    sib = me + 1 - 2 * (me % 2)
    zpeer = (me + 2) % 4
    places = 64

    def logical(layer, at):
        return jnp.where(at < 2, layer, 3 - layer)

    def layer_of(ll):
        return jnp.where(low, ll, 3 - ll)

    mine = logical(me, me)

    has = {DOWN: p > 0, UP: p < places - 1}
    gets = {DOWN: p < places - 1, UP: p > 0}
    step = {DOWN: -1, UP: 1}
    cross = {
        DOWN: (p % 16 == 0) & (p > 0),
        UP: (p % 16 == 15) & (p < places - 1),
    }
    via = {DOWN: p + 15, UP: p - 15}
    relays = {
        DOWN: (p % 16 == 15) & (p >= 16),
        UP: (p % 16 == 0) & (p < places - 16),
    }
    relay_from = {DOWN: p - 15, UP: p + 15}
    relay_to = {DOWN: p - 16, UP: p + 16}
    crossed = {DOWN: (p % 16 == 15) & (p < places - 1), UP: (p % 16 == 0) & (p > 0)}
    crossed_via = {DOWN: p + 16, UP: p - 16}
    side = {DOWN: 2, UP: 0}

    def cl(x):
        return jnp.clip(x, 0, places - 1)

    def rows(ll, j):
        return pl.ds(pl.multiple_of((ll * 3 + j) * CELL, CELL), CELL)

    def cols(t):
        return pl.ds(pl.multiple_of(t * GW, GW), GW)

    def cell(ll):
        return pl.ds(pl.multiple_of(ll * CELL, CELL), CELL)

    def remote(src, dst, ss, rs, dz, place):
        return pltpu.make_async_remote_copy(
            src_ref=src, dst_ref=dst, send_sem=ss, recv_sem=rs,
            device_id=(dz, place), device_id_type=MESH,
        )

    own = cols(me)
    loads = [
        pltpu.make_async_copy(k_hbm.at[:, own], kv.at[0, rows(mine, 1)], loc.at[0]),
        pltpu.make_async_copy(v_hbm.at[:, own], kv.at[1, rows(mine, 1)], loc.at[1]),
        pltpu.make_async_copy(q_hbm.at[:, own], qs.at[cell(mine)], loc.at[2]),
        pltpu.make_async_copy(g_hbm, graw, loc.at[3]),
        pltpu.make_async_copy(w_hbm.at[:, own], ww, loc.at[4]),
    ]
    for c in loads:
        c.start()

    u, x = p // 4, p % 4
    peers = []
    for e in range(1, 16):
        peers.append((None, me, ((u + e) % 16) * 4 + x))
    at = me * 4 + x
    for e in range(1, 16):
        to = (at + e) % 16
        peers.append((None, to // 4, u * 4 + to % 4))
    for d in (DOWN, UP):
        peers.append((has[d], me, cl(p + step[d])))
        peers.append((cross[d], me, cl(via[d])))
        peers.append((relays[d], me, cl(relay_from[d])))
        peers.append((relays[d], me, cl(relay_to[d])))
        peers.append((crossed[d], me, cl(crossed_via[d])))
    barrier = pltpu.get_barrier_semaphore()
    expect = 0
    for ok, a, b in peers:

        def greet(a=a, b=b):
            pl.semaphore_signal(barrier, inc=1, device_id=(a, b), device_id_type=MESH)

        if ok is None:
            greet()
            expect = expect + 1
        else:
            pl.when(ok)(greet)
            expect = expect + jnp.where(ok, 1, 0)

    lane = lax.broadcasted_iota(jnp.int32, (8, 128), 1)
    plain = jnp.zeros((8, 128), jnp.int32)
    turned = jnp.zeros((8, 128), jnp.int32)
    for s in range(9):
        plain = jnp.where(lane == s, pair_ref[0, s], plain)
        turned = jnp.where(lane == (2 - s // 3) * 3 + s % 3, pair_ref[0, s], turned)
    pcs[0] = plain
    pcs[1] = turned
    pc[mine] = jnp.where(low, plain, turned)

    def clear(d):
        for ll in range(4):
            kv[:, (ll * 3 + side[d]) * CELL : (ll * 3 + side[d] + 1) * CELL, :] = (
                jnp.zeros((2, CELL, GW), BF)
            )
            got[d, ll] = jnp.zeros((2, CELL, GW), BF)

    for d in (DOWN, UP):
        pl.when(jnp.logical_not(gets[d]))(lambda d=d: clear(d))

    pl.semaphore_wait(barrier, expect)

    def spread(kind, o):
        t = (me + o) % 4
        lt = logical(me, t)
        if kind == C_:
            turn = jnp.where(t < 2, 0, 1)
            return remote(pcs.at[turn], pc.at[lt], a_s.at[C_, o], a_r.at[C_, lt], t, p)
        src = (k_hbm, v_hbm, q_hbm)[kind].at[:, cols(t)]
        dst = kv.at[kind, rows(lt, 1)] if kind != Q_ else qs.at[cell(lt)]
        return remote(src, dst, a_s.at[kind, o], a_r.at[kind, lt], t, p)

    def arrived(kind, ll):
        if kind == C_:
            dst = pc.at[ll]
        elif kind == G_:
            dst = gm.at[cell(ll)]
        elif kind == Q_:
            dst = qs.at[cell(ll)]
        else:
            dst = kv.at[kind, rows(ll, 1)]
        remote(dst, dst, a_s.at[kind, 0], a_r.at[kind, ll], sib, p).wait_recv()

    for kind in (K_, V_):
        for o in (1, 3, 2):
            spread(kind, o).start()

    def halo(d, ll, kind, place=None):
        blk = kv.at[kind, rows(ll, 1)]
        dst = kv.at[kind, rows(ll, side[d])]
        return remote(
            blk, dst, b_s.at[d, ll, kind], b_r.at[d, ll, kind], me, cl(p + step[d])
        )

    def halo_detour(d, ll):
        blk = kv.at[1, rows(ll, 1)]
        return remote(
            blk, hold.at[d, ll], b_s.at[d, ll, 1], l_r.at[d, ll], me, cl(via[d])
        )

    def halo_forward(d, ll):
        dst = kv.at[1, rows(ll, side[d])]
        return remote(
            hold.at[d, ll], dst, l_s.at[d, ll], b_r.at[d, ll, 1], me, cl(relay_to[d])
        )

    def send_halo(ll, kind):
        for d in (UP, DOWN):
            if kind == 0:
                pl.when(has[d])(lambda d=d: halo(d, ll, 0).start())
            else:
                pl.when(has[d] & jnp.logical_not(cross[d]))(
                    lambda d=d: halo(d, ll, 1).start()
                )
                pl.when(cross[d])(lambda d=d: halo_detour(d, ll).start())

    def forward_halo(ll):
        for d in (UP, DOWN):

            def go(d=d):
                halo_detour(d, ll).wait_recv()
                halo_forward(d, ll).start()

            pl.when(relays[d])(go)

    loads[0].wait()
    send_halo(mine, 0)
    loads[1].wait()
    send_halo(mine, 1)
    other = 1 - mine
    for kind in (0, 1):
        arrived(kind, other)
        send_halo(other, kind)

    for kind in (Q_, C_):
        for o in (3, 2, 1):
            spread(kind, o).start()

    loads[3].wait()
    live = lax.broadcasted_iota(jnp.int32, (CELL, 1024), 0) < count_ref[0]
    gown[...] = jnp.where(live, graw[...], jnp.zeros((CELL, 1024), BF))
    own_g = pltpu.make_async_copy(gown, gm.at[cell(mine)], loc.at[5])
    own_g.start()

    def g_to(t, o):
        lt = logical(me, t)
        return remote(gown, gm.at[cell(lt)], a_s.at[G_, o], a_r.at[G_, lt], t, p)

    zl = logical(zpeer, me)
    g_sib = g_to(sib, 1)
    g_z = g_to(zpeer, 2)
    g_fwd = remote(
        gm.at[cell(zl)], gm.at[cell(zl)], a_s.at[G_, 3], a_r.at[G_, zl], sib, p
    )
    g_z.start()
    g_sib.start()

    for ll in (2, 3):
        for kind in (0, 1):
            arrived(kind, ll)
            send_halo(ll, kind)

    arrived(G_, zl)
    g_fwd.start()

    forward_halo(0)
    forward_halo(1)
    forward_halo(2)
    forward_halo(3)

    loads[4].wait()
    own_g.wait()
    arrived(G_, other)
    arrived(G_, 5 - zl)
    for ll in range(4):
        do[cell(ll)] = dot(gm[cell(ll)], ww[...]).astype(BF)

    loads[2].wait()
    for kind in (Q_, C_):
        arrived(kind, other)
        arrived(kind, 2)
        arrived(kind, 3)
    for ll in range(4):
        qs[cell(ll)] = qs[cell(ll)] * jnp.asarray(0.125, BF)

    def halo_arrived(ll):
        for d in (UP, DOWN):
            for kind in (0, 1):
                pl.when(gets[d])(lambda d=d, kind=kind: halo(d, ll, kind).wait_recv())

    def turn_layer(ll):
        for j in range(3):
            for kind in (0, 1):
                at_ = (ll * 3 + j) * CELL
                kvt[kind, :, at_ : at_ + CELL] = kv[kind, at_ : at_ + CELL, :].T

    first = [0, 0, 1, 2]
    last = [1, 2, 3, 3]
    base = [0, 768, 1920, 3072]
    sub = lax.broadcasted_iota(jnp.int32, (CELL, 128), 0)

    def fold(op, v):
        return op(v.reshape(CELL // 8, 8, 256), axis=0)

    def forward(lq):
        bias = jnp.where(sub < pc[lq][0:1, :], 0.0, NEG)
        slots = [(ll, j) for ll in range(first[lq], last[lq] + 1) for j in range(3)]
        n = len(slots) * CELL
        r0 = first[lq] * 3 * CELL
        cq = slice(lq * CELL, (lq + 1) * CELL)
        for hp in range(2):
            hc = slice(hp * 128, hp * 128 + 128)
            qt = halves_t(qs[cq, hc].T)
            top = None
            for i, (ll, j) in enumerate(slots):
                at_ = (ll * 3 + j) * CELL
                k9 = (ll - lq + 1) * 3 + j
                s = dot(kv[0, at_ : at_ + CELL, hc], qt) + bias[:, k9 : k9 + 1]
                sbuf[i * CELL : (i + 1) * CELL, :] = s
                t = fold(jnp.max, s)
                top = t if top is None else jnp.maximum(top, t)
            top = jnp.max(top, axis=0, keepdims=True)
            total = None
            b0 = base[lq]
            for i in range(len(slots)):
                e = jnp.exp(sbuf[i * CELL : (i + 1) * CELL, :] - top)
                pbuf[hp, b0 + i * CELL : b0 + (i + 1) * CELL, :] = e.astype(BF)
                t = fold(jnp.sum, e)
                total = t if total is None else total + t
            inv = 1.0 / jnp.sum(total, axis=0, keepdims=True)
            at_t = dot(kvt[1, hc, r0 : r0 + n], pbuf[hp, b0 : b0 + n, :])
            at_t = diagonal(at_t * inv).astype(BF)
            att[cq, hc] = at_t.T
            inv2 = jnp.concatenate(
                [
                    jnp.broadcast_to(inv[:, :128], (64, 128)),
                    jnp.broadcast_to(inv[:, 128:], (64, 128)),
                ],
                axis=0,
            )
            dt = (do[cq, hc].T.astype(F32) * inv2).astype(BF)
            dos[lq, hp] = dt
            prod = dt.astype(F32) * at_t.astype(F32)
            dl = jnp.concatenate(
                [
                    jnp.sum(prod[:64], axis=0, keepdims=True),
                    jnp.sum(prod[64:], axis=0, keepdims=True),
                ],
                axis=1,
            )
            delta[lq, hp] = jnp.broadcast_to(dl, (8, 256))

    def backward(lq):
        slots = [(ll, j) for ll in range(first[lq], last[lq] + 1) for j in range(3)]
        n = len(slots) * CELL
        r0 = first[lq] * 3 * CELL
        cq = slice(lq * CELL, (lq + 1) * CELL)
        b0 = base[lq]
        for hp in range(2):
            hc = slice(hp * 128, hp * 128 + 128)
            dt = dos[lq, hp]
            dmt = halves_t(dt)
            dm = halves(dt.T)
            qm = halves(qs[cq, hc])
            dl = delta[lq, hp][0:1, :]
            for i, (ll, j) in enumerate(slots):
                at_ = (ll * 3 + j) * CELL
                pr = pbuf[hp, b0 + i * CELL : b0 + (i + 1) * CELL, :]
                dp = dot(kv[1, at_ : at_ + CELL, hc], dmt)
                ds = (pr.astype(F32) * (dp - dl)).astype(BF)
                dsb[i * CELL : (i + 1) * CELL, :] = ds
                dv = dot(pr, dm)
                dk = dot(ds, qm)
                if lq == max(ll - 1, 0):
                    acc[1, at_ : at_ + CELL, hc] = dv
                    acc[0, at_ : at_ + CELL, hc] = dk
                else:
                    acc[1, at_ : at_ + CELL, hc] += dv
                    acc[0, at_ : at_ + CELL, hc] += dk
            dqt = dot(kvt[0, hc, r0 : r0 + n], dsb[0:n, :])
            dqs[cq, hc] = (diagonal(dqt) * 0.125).T.astype(BF)

    def part(d, ll, kind):
        return remote(
            back.at[d, ll, kind], got.at[d, ll, kind],
            d_s.at[d, ll, kind], d_r.at[d, ll, kind], me, cl(p + step[d]),
        )

    def part_detour(d, ll):
        return remote(
            back.at[d, ll, 1], hold2.at[d, ll],
            d_s.at[d, ll, 1], m_r.at[d, ll], me, cl(via[d]),
        )

    def part_forward(d, ll):
        return remote(
            hold2.at[d, ll], got.at[d, ll, 1],
            m_s.at[d, ll], d_r.at[d, ll, 1], me, cl(relay_to[d]),
        )

    def send_parts(ll):
        for d in (UP, DOWN):
            j = 2 if d == UP else 0
            at_ = (ll * 3 + j) * CELL
            for kind in (1, 0):
                back[d, ll, kind] = acc[kind, at_ : at_ + CELL, :].astype(BF)

            def near(d=d):
                part(d, ll, 1).start()

            def detour(d=d):
                part_detour(d, ll).start()

            def keys(d=d):
                part(d, ll, 0).start()

            pl.when(has[d] & jnp.logical_not(cross[d]))(near)
            pl.when(cross[d])(detour)
            pl.when(has[d])(keys)

    def forward_parts(ll):
        for d in (UP, DOWN):

            def go(d=d):
                part_detour(d, ll).wait_recv()
                part_forward(d, ll).start()

            pl.when(relays[d])(go)

    def home(kind, ll, src):
        t = layer_of(ll)
        out = (dk_hbm, dv_hbm, dq_hbm)[kind].at[:, cols(me)]
        o = (t - me + 4) % 4
        far = remote(src, out, f_s.at[kind, ll], f_r.at[kind, o], t, p)
        near = pltpu.make_async_copy(src, out, f_s.at[kind, ll])
        return far, near

    def send_home(kind, ll, src):
        far, near = home(kind, ll, src)
        if ll >= 2:
            far.start()
        else:
            pl.when(mine != ll)(lambda: far.start())
            pl.when(mine == ll)(lambda: near.start())

    def sent_home(kind, ll, src):
        far, near = home(kind, ll, src)
        if ll >= 2:
            far.wait_send()
        else:
            pl.when(mine != ll)(lambda: far.wait_send())
            pl.when(mine == ll)(lambda: near.wait())

    def finish(ll):
        for d in (UP, DOWN):
            for kind in (0, 1):
                pl.when(gets[d])(lambda d=d, kind=kind: part(d, ll, kind).wait_recv())
        at_ = (ll * 3 + 1) * CELL
        for kind in (0, 1):
            s = acc[kind, at_ : at_ + CELL, :]
            s = s + got[0, ll, kind].astype(F32) + got[1, ll, kind].astype(F32)
            fin[kind, ll] = s.astype(BF)
            send_home(kind, ll, fin.at[kind, ll])

    halo_arrived(0)
    turn_layer(0)
    halo_arrived(1)
    turn_layer(1)
    forward(0)
    backward(0)
    send_home(2, 0, dqs.at[cell(0)])
    halo_arrived(2)
    turn_layer(2)
    forward(1)
    backward(1)
    send_home(2, 1, dqs.at[cell(1)])
    send_parts(0)
    halo_arrived(3)
    turn_layer(3)
    forward(2)
    forward(3)

    wsum[...] = lax.dot_general(
        gm[...], att[...], (((0,), (0,)), ((), ())), preferred_element_type=F32
    ).astype(BF)

    def stage1(e):
        to = (u + e) % 16
        return remote(
            wsum.at[pl.ds(pl.multiple_of(to * 64, 64), 64)], wgot.at[e],
            u_s.at[e], u_r.at[e], me, to * 4 + x,
        )

    for e in range(1, 16):
        stage1(e).start()
    forward_parts(0)
    backward(2)
    send_home(2, 2, dqs.at[cell(2)])
    send_parts(1)
    backward(3)
    send_home(2, 3, dqs.at[cell(3)])
    send_parts(2)
    send_parts(3)
    forward_parts(1)
    forward_parts(2)
    forward_parts(3)

    mine_w = wsum[pl.ds(pl.multiple_of(u * 64, 64), 64), :].astype(F32)
    for e in range(1, 16):
        stage1(e).wait_recv()
        mine_w = mine_w + wgot[e].astype(F32)
    x2[...] = mine_w

    def stage2(e):
        to = (at + e) % 16
        return remote(
            x2.at[pl.ds(pl.multiple_of((to % 4) * 16, 16), 16)],
            xgot.at[x, :, cols(me)],
            x_s.at[e], x_r.at[e], to // 4, u * 4 + to % 4,
        )

    for e in range(1, 16):
        stage2(e).start()
    own_x = pltpu.make_async_copy(
        x2.at[pl.ds(pl.multiple_of(x * 16, 16), 16)], xgot.at[x, :, cols(me)], loc.at[6]
    )
    own_x.start()

    finish(0)
    finish(1)
    finish(2)
    finish(3)

    own_x.wait()
    for e in range(1, 16):
        came = (at - e + 16) % 16
        spot = xgot.at[came % 4, :, cols(came // 4)]
        remote(spot, spot, x_s.at[e], x_r.at[e], sib, p).wait_recv()
    wo_ref[...] = (xgot[0] + xgot[1] + xgot[2] + xgot[3]) * (32768 ** -0.5)

    for kind in range(3):
        for o in range(1, 4):
            spot = (dk_hbm, dv_hbm, dq_hbm)[kind].at[:, cols((me - o + 4) % 4)]
            remote(spot, spot, f_s.at[kind, 0], f_r.at[kind, o], sib, p).wait_recv()
    for ll in range(4):
        sent_home(0, ll, fin.at[0, ll])
        sent_home(1, ll, fin.at[1, ll])
        sent_home(2, ll, dqs.at[cell(ll)])
    for kind in (K_, V_, Q_, C_):
        for o in (1, 2, 3):
            spread(kind, o).wait_send()
    g_sib.wait_send()
    g_z.wait_send()
    g_fwd.wait_send()
    for e in range(1, 16):
        stage1(e).wait_send()
        stage2(e).wait_send()
    for ll in range(4):
        for d in (UP, DOWN):

            def sent(d=d):
                halo(d, ll, 0).wait_send()
                halo(d, ll, 1).wait_send()
                part(d, ll, 0).wait_send()
                part(d, ll, 1).wait_send()

            def relayed(d=d):
                halo_forward(d, ll).wait_send()
                part_forward(d, ll).wait_send()

            pl.when(has[d])(sent)
            pl.when(relays[d])(relayed)


def shards(queries, keys, values, out_grad, out_weight, pair_counts, counts):
    n, width = queries.shape
    big = pl.BlockSpec(memory_space=pl.ANY)
    small = pl.BlockSpec(memory_space=pltpu.SMEM)
    dma = pltpu.SemaphoreType.DMA
    wide = jax.ShapeDtypeStruct((n, width), BF)
    return pl.pallas_call(
        kernel,
        name="cell_attention_backward",
        out_shape=(wide, wide, wide, jax.ShapeDtypeStruct((16, width), F32)),
        in_specs=[big] * 5 + [small] * 2,
        out_specs=(big, big, big, pl.BlockSpec(memory_space=pltpu.VMEM)),
        scratch_shapes=[
            pltpu.VMEM((2, 1536, GW), BF),
            pltpu.VMEM((2, GW, 1536), BF),
            pltpu.VMEM((512, GW), BF),
            pltpu.VMEM((512, 1024), BF),
            pltpu.VMEM((CELL, 1024), BF),
            pltpu.VMEM((CELL, 1024), BF),
            pltpu.VMEM((1024, GW), BF),
            pltpu.VMEM((512, GW), BF),
            pltpu.VMEM((4, 8, 128), jnp.int32),
            pltpu.VMEM((2, 8, 128), jnp.int32),
            pltpu.VMEM((1152, 256), F32),
            pltpu.VMEM((2, 3840, 256), BF),
            pltpu.VMEM((1152, 256), BF),
            pltpu.VMEM((4, 2, 128, 128), BF),
            pltpu.VMEM((4, 2, 8, 256), F32),
            pltpu.VMEM((512, GW), BF),
            pltpu.VMEM((2, 1536, GW), F32),
            pltpu.VMEM((512, GW), BF),
            pltpu.VMEM((2, 4, CELL, GW), BF),
            pltpu.VMEM((2, 4, 2, CELL, GW), BF),
            pltpu.VMEM((2, 4, 2, CELL, GW), BF),
            pltpu.VMEM((2, 4, CELL, GW), BF),
            pltpu.VMEM((2, 4, CELL, GW), BF),
            pltpu.VMEM((1024, GW), BF),
            pltpu.VMEM((16, 64, GW), BF),
            pltpu.VMEM((64, GW), F32),
            pltpu.VMEM((4, 16, 1024), F32),
            dma((7,)),
            dma((5, 4)),
            dma((5, 4)),
            dma((2, 4, 2)),
            dma((2, 4, 2)),
            dma((2, 4)),
            dma((2, 4)),
            dma((2, 4, 2)),
            dma((2, 4, 2)),
            dma((2, 4)),
            dma((2, 4)),
            dma((3, 4)),
            dma((3, 4)),
            dma((16,)),
            dma((16,)),
            dma((16,)),
            dma((16,)),
        ],
        compiler_params=pltpu.CompilerParams(
            collective_id=0, has_side_effects=True, vmem_limit_bytes=48 * 2**20
        ),
        cost_estimate=pl.CostEstimate(
            flops=3_000_000_000, bytes_accessed=4_000_000, transcendentals=2_000_000
        ),
    )(queries, keys, values, out_grad, out_weight, pair_counts, counts)


def solution(mesh):
    both = P(("dz", "dxy"), None)
    return jax.shard_map(
        shards,
        mesh=mesh,
        in_specs=(both, both, both, both, P(), both, P(("dz", "dxy"))),
        out_specs=(both, both, both, P("dxy", None)),
        check_vma=False,
    )
```

```python
import jax
import jax.numpy as jnp
from jax import lax
from jax.experimental import pallas as pl
from jax.experimental.pallas import tpu as pltpu
from jax.sharding import PartitionSpec as P

MESH = pl.DeviceIdType.MESH
BF = jnp.bfloat16
F32 = jnp.float32
CELL = 128
GW = 256
DOWN, UP = 0, 1
K_, V_, Q_, D_, G_, C_ = 0, 1, 2, 3, 4, 5
WAY = {(0, 0): 1, (0, 1): 2, (1, 0): 3, (1, 1): 0, (2, 0): 1, (2, 1): 2, (3, 0): 3, (3, 1): 0}
VIA = {1: -15, 2: -3, 3: -12}
ONTO = {1: 16, 2: 4, 3: 13}
NEG = -1e30


def dot(a, b):
    return jnp.dot(a, b, preferred_element_type=F32)


def halves_t(x):
    row = lax.broadcasted_iota(jnp.int32, x.shape, 0)
    zero = jnp.zeros_like(x)
    return jnp.concatenate(
        [jnp.where(row < 64, x, zero), jnp.where(row < 64, zero, x)], axis=1
    )


def halves(x):
    lane = lax.broadcasted_iota(jnp.int32, x.shape, 1)
    zero = jnp.zeros_like(x)
    return jnp.concatenate(
        [jnp.where(lane < 64, x, zero), jnp.where(lane < 64, zero, x)], axis=0
    )


def diagonal(x):
    return jnp.concatenate([x[:64, :128], x[64:, 128:]], axis=0)


def kernel(
    q_hbm, k_hbm, v_hbm, g_hbm, w_hbm, pair_ref, count_ref,
    dq_hbm, dk_hbm, dv_hbm, wo_ref,
    kv, kvt, qs, gm, graw, gown, ww, dhome, do, pc, pcs,
    sbuf, pbuf, dsb, scale, att, acc, dqs,
    hold, back, got, hold2, fin, wsum, wgot, w2, w2got, w3, w3got,
    loc, a_s, a_r, b_s, b_r, l_s, l_r, d_s, d_r, m_s, m_r, f_s, f_r, u_s, u_r, x_s, x_r, y_s, y_r,
):
    me = lax.axis_index("dz")
    p = lax.axis_index("dxy")
    low = me < 2
    sib = me + 1 - 2 * (me % 2)
    zpeer = (me + 2) % 4
    zdiag = (sib + 2) % 4
    group = (sib, zpeer, zdiag)
    places = 64

    def logical(layer, at):
        return jnp.where(at < 2, layer, 3 - layer)

    def layer_of(ll):
        return jnp.where(low, ll, 3 - ll)

    mine = logical(me, me)

    has = {DOWN: p > 0, UP: p < places - 1}
    gets = {DOWN: p < places - 1, UP: p > 0}
    step = {DOWN: -1, UP: 1}
    cross = {
        DOWN: (p % 16 == 0) & (p > 0),
        UP: (p % 16 == 15) & (p < places - 1),
    }
    crossed = {DOWN: (p % 16 == 15) & (p < places - 1), UP: (p % 16 == 0) & (p > 0)}
    relays = {}
    for r in (1, 2, 3):
        relays[UP, r] = (p % 16 == (15 + VIA[r]) % 16) & (p - VIA[r] < places - 1)
        relays[DOWN, r] = (p % 16 == -VIA[r] % 16) & (p + VIA[r] > 0)

    def via(d, r):
        return cl(p + step[d] * VIA[r])

    def relay_from(d, r):
        return cl(p - step[d] * VIA[r])

    def relay_to(d, r):
        return cl(p + step[d] * ONTO[r])

    def crossed_via(d, r):
        return cl(p - step[d] * ONTO[r])

    side = {DOWN: 2, UP: 0}

    def cl(x):
        return jnp.clip(x, 0, places - 1)

    def rows(ll, j):
        return pl.ds(pl.multiple_of((ll * 3 + j) * CELL, CELL), CELL)

    def cols(t):
        return pl.ds(pl.multiple_of(t * GW, GW), GW)

    def cell(ll):
        return pl.ds(pl.multiple_of(ll * CELL, CELL), CELL)

    def remote(src, dst, ss, rs, dz, place):
        return pltpu.make_async_remote_copy(
            src_ref=src, dst_ref=dst, send_sem=ss, recv_sem=rs,
            device_id=(dz, place), device_id_type=MESH,
        )

    own = cols(me)
    loads = [
        pltpu.make_async_copy(k_hbm.at[:, own], kv.at[0, rows(mine, 1)], loc.at[0]),
        pltpu.make_async_copy(v_hbm.at[:, own], kv.at[1, rows(mine, 1)], loc.at[1]),
        pltpu.make_async_copy(q_hbm.at[:, own], qs.at[cell(mine)], loc.at[2]),
        pltpu.make_async_copy(g_hbm, graw, loc.at[3]),
        pltpu.make_async_copy(w_hbm, ww, loc.at[4]),
    ]
    for c in loads:
        c.start()

    zh, y, x = p // 16, (p // 4) % 4, p % 4
    at = zh * 4 + me

    def in_column(e):
        return zh * 16 + ((y + e) % 4) * 4 + x

    def in_row(e):
        return zh * 16 + y * 4 + (x + e) % 4

    def across(e):
        to = (at + e) % 16
        return to % 4, (to // 4) * 16 + y * 4 + x

    peers = []
    for e in range(1, 4):
        peers.append((None, me, in_column(e)))
        peers.append((None, me, in_row(e)))
    for e in range(1, 16):
        peers.append((None, *across(e)))
    for d in (DOWN, UP):
        peers.append((has[d], me, cl(p + step[d])))
        for r in (1, 2, 3):
            peers.append((cross[d], me, via(d, r)))
            peers.append((relays[d, r], me, relay_from(d, r)))
            peers.append((relays[d, r], me, relay_to(d, r)))
            peers.append((crossed[d], me, crossed_via(d, r)))
    barrier = pltpu.get_barrier_semaphore()
    expect = 0
    for ok, a, b in peers:

        def greet(a=a, b=b):
            pl.semaphore_signal(barrier, inc=1, device_id=(a, b), device_id_type=MESH)

        if ok is None:
            greet()
            expect = expect + 1
        else:
            pl.when(ok)(greet)
            expect = expect + jnp.where(ok, 1, 0)

    lane = lax.broadcasted_iota(jnp.int32, (8, 128), 1)
    plain = jnp.zeros((8, 128), jnp.int32)
    turned = jnp.zeros((8, 128), jnp.int32)
    for s in range(9):
        plain = jnp.where(lane == s, pair_ref[0, s], plain)
        turned = jnp.where(lane == (2 - s // 3) * 3 + s % 3, pair_ref[0, s], turned)
    pcs[0] = plain
    pcs[1] = turned
    pc[mine] = jnp.where(low, plain, turned)

    def clear(d):
        for ll in range(4):
            kv[:, (ll * 3 + side[d]) * CELL : (ll * 3 + side[d] + 1) * CELL, :] = (
                jnp.zeros((2, CELL, GW), BF)
            )
            got[d, ll] = jnp.zeros((2, CELL, GW), BF)

    for d in (DOWN, UP):
        pl.when(jnp.logical_not(gets[d]))(lambda d=d: clear(d))

    pl.semaphore_wait(barrier, expect)

    def landing(kind, ll):
        if kind == C_:
            return pc.at[ll]
        if kind in (K_, V_):
            return kv.at[kind, rows(ll, 1)]
        return {Q_: qs, D_: do, G_: gm}[kind].at[cell(ll)]

    def spread(kind, i):
        t = group[i]
        lt = logical(me, t)
        if kind == C_:
            src = pcs.at[jnp.where(t < 2, 0, 1)]
        elif kind == G_:
            src = gown
        else:
            src = {K_: k_hbm, V_: v_hbm, Q_: q_hbm, D_: dhome}[kind].at[:, cols(t)]
        return remote(
            src, landing(kind, lt), a_s.at[kind, i], a_r.at[kind, lt], t, p
        )

    def arrived(kind, ll):
        dst = landing(kind, ll)
        remote(dst, dst, a_s.at[kind, 0], a_r.at[kind, ll], sib, p).wait_recv()

    for kind in (K_, V_, C_, Q_):
        for i in range(3):
            spread(kind, i).start()

    def halo(d, ll, kind):
        blk = kv.at[kind, rows(ll, 1)]
        dst = kv.at[kind, rows(ll, side[d])]
        return remote(
            blk, dst, b_s.at[d, ll, kind], b_r.at[d, ll, kind], me, cl(p + step[d])
        )

    def halo_detour(d, ll, kind, r):
        blk = kv.at[kind, rows(ll, 1)]
        return remote(
            blk, hold.at[d, ll], b_s.at[d, ll, kind], l_r.at[d, ll], me, via(d, r)
        )

    def halo_forward(d, ll, kind, r):
        dst = kv.at[kind, rows(ll, side[d])]
        return remote(
            hold.at[d, ll], dst, l_s.at[d, ll], b_r.at[d, ll, kind], me, relay_to(d, r)
        )

    def part(d, ll, kind):
        return remote(
            back.at[d, ll, kind], got.at[d, ll, kind],
            d_s.at[d, ll, kind], d_r.at[d, ll, kind], me, cl(p + step[d]),
        )

    def part_detour(d, ll, kind, r):
        return remote(
            back.at[d, ll, kind], hold2.at[d, ll],
            d_s.at[d, ll, kind], m_r.at[d, ll], me, via(d, r),
        )

    def part_forward(d, ll, kind, r):
        return remote(
            hold2.at[d, ll], got.at[d, ll, kind],
            m_s.at[d, ll], d_r.at[d, ll, kind], me, relay_to(d, r),
        )

    def send_beside(pos, ll, kind, straight, detour):
        r = WAY[pos, kind]
        for d in (UP, DOWN):
            if r == 0:
                pl.when(has[d])(lambda d=d: straight(d, ll, kind).start())
            else:
                pl.when(has[d] & jnp.logical_not(cross[d]))(
                    lambda d=d: straight(d, ll, kind).start()
                )
                pl.when(cross[d])(lambda d=d: detour(d, ll, kind, r).start())

    def pass_on(pos, ll, detour, forward):
        for kind in (0, 1):
            r = WAY[pos, kind]
            if r == 0:
                continue
            for d in (UP, DOWN):

                def go(d=d):
                    detour(d, ll, kind, r).wait_recv()
                    forward(d, ll, kind, r).start()

                pl.when(relays[d, r])(go)

    def send_halo(pos, ll, kind):
        send_beside(pos, ll, kind, halo, halo_detour)

    def forward_halo(pos, ll):
        pass_on(pos, ll, halo_detour, halo_forward)

    other = 1 - mine
    loads[0].wait()
    send_halo(0, mine, 0)
    loads[1].wait()
    send_halo(0, mine, 1)
    for kind in (0, 1):
        arrived(kind, other)
        send_halo(1, other, kind)

    loads[3].wait()
    live = lax.broadcasted_iota(jnp.int32, (CELL, 1024), 0) < count_ref[0]
    gown[...] = jnp.where(live, graw[...], jnp.zeros((CELL, 1024), BF))
    own_g = pltpu.make_async_copy(gown, gm.at[cell(mine)], loc.at[5])
    own_g.start()
    spread(G_, 1).start()
    spread(G_, 0).start()
    loads[4].wait()
    for c in range(4):
        dhome[:, c * GW : (c + 1) * GW] = dot(
            gown[...], ww[:, c * GW : (c + 1) * GW]
        ).astype(BF)
    own_d = pltpu.make_async_copy(dhome.at[:, own], do.at[cell(mine)], loc.at[6])
    own_d.start()
    spread(D_, 0).start()

    forward_halo(0, mine)
    forward_halo(1, other)
    for kind in (0, 1):
        for ll in (2, 3):
            arrived(kind, ll)
            send_halo(ll, ll, kind)
    zl = logical(zpeer, me)
    g_fwd = remote(
        gm.at[cell(zl)], gm.at[cell(zl)], a_s.at[G_, 2], a_r.at[G_, zl], sib, p
    )

    def halo_arrived(ll):
        for d in (UP, DOWN):
            for kind in (0, 1):
                pl.when(gets[d])(lambda d=d, kind=kind: halo(d, ll, kind).wait_recv())

    def turn_layer(ll):
        for j in range(3):
            for kind in (0, 1):
                at_ = (ll * 3 + j) * CELL
                kvt[kind, :, at_ : at_ + CELL] = kv[kind, at_ : at_ + CELL, :].T

    first = [0, 0, 1, 2]
    last = [1, 2, 3, 3]
    base = [0, 768, 1920, 3072]
    sub = lax.broadcasted_iota(jnp.int32, (CELL, 128), 0)

    def fold(op, v):
        return op(v.reshape(CELL // 8, 8, 256), axis=0)

    def forward(lq):
        bias = jnp.where(sub < pc[lq][0:1, :], 0.0, NEG)
        slots = [(ll, j) for ll in range(first[lq], last[lq] + 1) for j in range(3)]
        n = len(slots) * CELL
        r0 = first[lq] * 3 * CELL
        cq = slice(lq * CELL, (lq + 1) * CELL)
        for hp in range(2):
            hc = slice(hp * 128, hp * 128 + 128)
            qt = halves_t((qs[cq, hc] * jnp.asarray(0.125, BF)).T)
            top = None
            for i, (ll, j) in enumerate(slots):
                at_ = (ll * 3 + j) * CELL
                k9 = (ll - lq + 1) * 3 + j
                s = dot(kv[0, at_ : at_ + CELL, hc], qt) + bias[:, k9 : k9 + 1]
                sbuf[i * CELL : (i + 1) * CELL, :] = s
                t = fold(jnp.max, s)
                top = t if top is None else jnp.maximum(top, t)
            top = jnp.max(top, axis=0, keepdims=True)
            total = None
            b0 = base[lq]
            for i in range(len(slots)):
                e = jnp.exp(sbuf[i * CELL : (i + 1) * CELL, :] - top)
                pbuf[hp, b0 + i * CELL : b0 + (i + 1) * CELL, :] = e.astype(BF)
                t = fold(jnp.sum, e)
                total = t if total is None else total + t
            inv = 1.0 / jnp.sum(total, axis=0, keepdims=True)
            at_t = dot(kvt[1, hc, r0 : r0 + n], pbuf[hp, b0 : b0 + n, :])
            att[hc, cq] = diagonal(at_t * inv).astype(BF)
            scale[lq, hp] = jnp.broadcast_to(inv, (8, 256))

    def backward(lq):
        slots = [(ll, j) for ll in range(first[lq], last[lq] + 1) for j in range(3)]
        n = len(slots) * CELL
        r0 = first[lq] * 3 * CELL
        cq = slice(lq * CELL, (lq + 1) * CELL)
        b0 = base[lq]
        for hp in range(2):
            hc = slice(hp * 128, hp * 128 + 128)
            inv = scale[lq, hp][0:1, :]
            inv = jnp.concatenate(
                [
                    jnp.broadcast_to(inv[:, :128], (64, 128)),
                    jnp.broadcast_to(inv[:, 128:], (64, 128)),
                ],
                axis=0,
            )
            dt = (do[cq, hc].T.astype(F32) * inv).astype(BF)
            prod = dt.astype(F32) * att[hc, cq].astype(F32)
            dl = jnp.concatenate(
                [
                    jnp.sum(prod[:64], axis=0, keepdims=True),
                    jnp.sum(prod[64:], axis=0, keepdims=True),
                ],
                axis=1,
            )
            dmt = halves_t(dt)
            dm = halves(dt.T)
            qm = halves(qs[cq, hc] * jnp.asarray(0.125, BF))
            for i, (ll, j) in enumerate(slots):
                at_ = (ll * 3 + j) * CELL
                pr = pbuf[hp, b0 + i * CELL : b0 + (i + 1) * CELL, :]
                dp = dot(kv[1, at_ : at_ + CELL, hc], dmt)
                ds = (pr.astype(F32) * (dp - dl)).astype(BF)
                dsb[i * CELL : (i + 1) * CELL, :] = ds
                dv = dot(pr, dm)
                dk = dot(ds, qm)
                if lq == max(ll - 1, 0):
                    acc[1, at_ : at_ + CELL, hc] = dv
                    acc[0, at_ : at_ + CELL, hc] = dk
                else:
                    acc[1, at_ : at_ + CELL, hc] += dv
                    acc[0, at_ : at_ + CELL, hc] += dk
            dqt = dot(kvt[0, hc, r0 : r0 + n], dsb[0:n, :])
            dqs[cq, hc] = (diagonal(dqt) * 0.125).T.astype(BF)

    def send_parts(ll):
        for d in (UP, DOWN):
            j = 2 if d == UP else 0
            at_ = (ll * 3 + j) * CELL
            for kind in (1, 0):
                back[d, ll, kind] = acc[kind, at_ : at_ + CELL, :].astype(BF)
        for kind in (1, 0):
            send_beside(ll, ll, kind, part, part_detour)

    def forward_parts(ll):
        pass_on(ll, ll, part_detour, part_forward)

    def home(kind, ll, src):
        t = layer_of(ll)
        out = (dk_hbm, dv_hbm, dq_hbm)[kind].at[:, cols(me)]
        o = (t - me + 4) % 4
        return remote(src, out, f_s.at[kind, ll], f_r.at[kind, o], t, p)

    def keep(kind, ll, src):
        out = (dk_hbm, dv_hbm, dq_hbm)[kind].at[:, cols(me)]
        return pltpu.make_async_copy(src, out, f_s.at[kind, ll])

    def send_home(kind, ll, src):
        if ll >= 2:
            home(kind, ll, src).start()
        else:
            pl.when(mine != ll)(lambda: home(kind, ll, src).start())
            pl.when(mine == ll)(lambda: keep(kind, ll, src).start())

    def sent_home(kind, ll, src):
        if ll >= 2:
            home(kind, ll, src).wait_send()
        else:
            pl.when(mine != ll)(lambda: home(kind, ll, src).wait_send())
            pl.when(mine == ll)(lambda: keep(kind, ll, src).wait())

    def finish(ll):
        for d in (UP, DOWN):
            for kind in (0, 1):
                pl.when(gets[d])(lambda d=d, kind=kind: part(d, ll, kind).wait_recv())
        at_ = (ll * 3 + 1) * CELL
        for kind in (0, 1):
            s = acc[kind, at_ : at_ + CELL, :]
            s = s + got[0, ll, kind].astype(F32) + got[1, ll, kind].astype(F32)
            fin[kind, ll] = s.astype(BF)
            send_home(kind, ll, fin.at[kind, ll])

    def stage1(e):
        return remote(
            wsum.at[:, (y + e) % 4], wgot.at[e], u_s.at[e], u_r.at[e], me, in_column(e)
        )

    def stage2(e):
        return remote(
            w2.at[:, (x + e) % 4], w2got.at[e], y_s.at[e], y_r.at[e], me, in_row(e)
        )

    def stage3(e):
        t, place = across(e)
        to = (at + e) % 16
        return remote(
            w3.at[to // 4], w3got.at[zh, :, cols(me)], x_s.at[e], x_r.at[e], t, place
        )

    loads[2].wait()
    own_d.wait()
    for kind in (C_, Q_, D_):
        arrived(kind, other)
    halo_arrived(0)
    turn_layer(0)
    halo_arrived(1)
    turn_layer(1)
    forward(0)
    spread(D_, 1).start()
    spread(D_, 2).start()
    forward_halo(2, 2)
    forward_halo(3, 3)
    backward(0)
    send_home(2, 0, dqs.at[cell(0)])
    halo_arrived(2)
    turn_layer(2)
    forward(1)
    backward(1)
    send_parts(0)
    send_home(2, 1, dqs.at[cell(1)])
    for kind in (C_, Q_):
        arrived(kind, 2)
        arrived(kind, 3)
    halo_arrived(3)
    turn_layer(3)
    forward(2)
    arrived(G_, zl)
    g_fwd.start()
    forward(3)
    own_g.wait()
    arrived(G_, other)
    arrived(G_, 5 - zl)
    for i in range(4):
        w_t = dot(att[...], gm[:, i * 256 : (i + 1) * 256]).astype(BF)
        wsum[i] = w_t.T.reshape(4, 64, GW)
    for e in range(1, 4):
        stage1(e).start()
    arrived(D_, 2)
    arrived(D_, 3)
    backward(2)
    send_parts(1)
    send_home(2, 2, dqs.at[cell(2)])
    forward_parts(0)
    backward(3)
    send_parts(2)
    send_parts(3)
    send_home(2, 3, dqs.at[cell(3)])
    finish(0)

    s1 = wsum[:, y].astype(F32)
    for e in range(1, 4):
        stage1(e).wait_recv()
        s1 = s1 + wgot[e].astype(F32)
    w2[...] = s1.astype(BF).reshape(4, 4, 16, GW)
    for e in range(1, 4):
        stage2(e).start()
    forward_parts(1)
    finish(1)
    forward_parts(2)

    s2 = w2[:, x].astype(F32)
    for e in range(1, 4):
        stage2(e).wait_recv()
        s2 = s2 + w2got[e].astype(F32)
    w3[...] = s2.astype(BF)
    for e in range(1, 16):
        stage3(e).start()
    own_x = pltpu.make_async_copy(w3.at[zh], w3got.at[zh, :, cols(me)], loc.at[7])
    own_x.start()
    forward_parts(3)
    finish(2)
    finish(3)
    own_x.wait()
    for e in range(1, 16):
        came = (at - e + 16) % 16
        spot = w3got.at[came // 4, :, cols(came % 4)]
        remote(spot, spot, x_s.at[e], x_r.at[e], sib, p).wait_recv()
    total = w3got[0].astype(F32)
    for i in range(1, 4):
        total = total + w3got[i].astype(F32)
    wo_ref[...] = total * (32768**-0.5)

    for kind in range(3):
        for o in range(1, 4):
            spot = (dk_hbm, dv_hbm, dq_hbm)[kind].at[:, cols((me - o + 4) % 4)]
            remote(spot, spot, f_s.at[kind, 0], f_r.at[kind, o], sib, p).wait_recv()
    for ll in range(4):
        sent_home(0, ll, fin.at[0, ll])
        sent_home(1, ll, fin.at[1, ll])
        sent_home(2, ll, dqs.at[cell(ll)])
    for kind in (K_, V_, Q_, D_, C_):
        for i in range(3):
            spread(kind, i).wait_send()
    spread(G_, 0).wait_send()
    spread(G_, 1).wait_send()
    g_fwd.wait_send()
    for e in range(1, 4):
        stage1(e).wait_send()
        stage2(e).wait_send()
    for e in range(1, 16):
        stage3(e).wait_send()
    for d in (UP, DOWN):

        def sent(d=d):
            for ll in range(4):
                for kind in (0, 1):
                    halo(d, ll, kind).wait_send()
                    part(d, ll, kind).wait_send()

        pl.when(has[d])(sent)
        for pos, ll in enumerate((mine, other, 2, 3)):
            for kind in (0, 1):
                r = WAY[pos, kind]
                if r:
                    pl.when(relays[d, r])(
                        lambda d=d: halo_forward(d, ll, kind, r).wait_send()
                    )
                r = WAY[pos, kind]
                if r:
                    pl.when(relays[d, r])(
                        lambda d=d: part_forward(d, pos, kind, r).wait_send()
                    )


def shards(queries, keys, values, out_grad, out_weight, pair_counts, counts):
    n, width = queries.shape
    big = pl.BlockSpec(memory_space=pltpu.HBM)
    small = pl.BlockSpec(memory_space=pltpu.SMEM)
    dma = pltpu.SemaphoreType.DMA
    wide = jax.ShapeDtypeStruct((n, width), BF)
    return pl.pallas_call(
        kernel,
        name="cell_attention_backward",
        out_shape=(wide, wide, wide, jax.ShapeDtypeStruct((16, width), F32)),
        in_specs=[big] * 5 + [small] * 2,
        out_specs=(big, big, big, pl.BlockSpec(memory_space=pltpu.VMEM)),
        scratch_shapes=[
            pltpu.VMEM((2, 1536, GW), BF),
            pltpu.VMEM((2, GW, 1536), BF),
            pltpu.VMEM((512, GW), BF),
            pltpu.VMEM((512, 1024), BF),
            pltpu.VMEM((CELL, 1024), BF),
            pltpu.VMEM((CELL, 1024), BF),
            pltpu.VMEM((1024, 1024), BF),
            pltpu.VMEM((CELL, 1024), BF),
            pltpu.VMEM((512, GW), BF),
            pltpu.VMEM((4, 8, 128), jnp.int32),
            pltpu.VMEM((2, 8, 128), jnp.int32),
            pltpu.VMEM((1152, 256), F32),
            pltpu.VMEM((2, 3840, 256), BF),
            pltpu.VMEM((1152, 256), BF),
            pltpu.VMEM((4, 2, 8, 256), F32),
            pltpu.VMEM((GW, 512), BF),
            pltpu.VMEM((2, 1536, GW), F32),
            pltpu.VMEM((512, GW), BF),
            pltpu.VMEM((2, 4, CELL, GW), BF),
            pltpu.VMEM((2, 4, 2, CELL, GW), BF),
            pltpu.VMEM((2, 4, 2, CELL, GW), BF),
            pltpu.VMEM((2, 4, CELL, GW), BF),
            pltpu.VMEM((2, 4, CELL, GW), BF),
            pltpu.VMEM((4, 4, 64, GW), BF),
            pltpu.VMEM((4, 4, 64, GW), BF),
            pltpu.VMEM((4, 4, 16, GW), BF),
            pltpu.VMEM((4, 4, 16, GW), BF),
            pltpu.VMEM((4, 16, GW), BF),
            pltpu.VMEM((4, 16, 1024), BF),
            dma((8,)),
            dma((6, 4)),
            dma((6, 4)),
            dma((2, 4, 2)),
            dma((2, 4, 2)),
            dma((2, 4)),
            dma((2, 4)),
            dma((2, 4, 2)),
            dma((2, 4, 2)),
            dma((2, 4)),
            dma((2, 4)),
            dma((3, 4)),
            dma((3, 4)),
            dma((4,)),
            dma((4,)),
            dma((16,)),
            dma((16,)),
            dma((4,)),
            dma((4,)),
        ],
        compiler_params=pltpu.CompilerParams(
            collective_id=0, has_side_effects=True, vmem_limit_bytes=53 * 2**20
        ),
        cost_estimate=pl.CostEstimate(
            flops=3_000_000_000, bytes_accessed=4_000_000, transcendentals=2_000_000
        ),
    )(queries, keys, values, out_grad, out_weight, pair_counts, counts)


def solution(mesh):
    both = P(("dz", "dxy"), None)
    return jax.shard_map(
        shards,
        mesh=mesh,
        in_specs=(both, both, both, both, P(), both, P(("dz", "dxy"))),
        out_specs=(both, both, both, P("dxy", None)),
        check_vma=False,
    )
```

```python
import jax
import jax.numpy as jnp
from jax import lax
from jax.experimental import pallas as pl
from jax.experimental.pallas import tpu as pltpu
from jax.sharding import PartitionSpec as P

MESH = pl.DeviceIdType.MESH
BF = jnp.bfloat16
F32 = jnp.float32
CELL = 128
GW = 256
DOWN, UP = 0, 1
K_, V_, Q_, G_, C_ = 0, 1, 2, 3, 4
WAY = {(0, 0): 1, (0, 1): 2, (1, 0): 3, (1, 1): 0, (2, 0): 1, (2, 1): 2, (3, 0): 3, (3, 1): 0}
VIA = {1: -15, 2: -3, 3: -12}
ONTO = {1: 16, 2: 4, 3: 13}
NEG = -1e30


def dot(a, b):
    return jnp.dot(a, b, preferred_element_type=F32)


def halves_t(x):
    row = lax.broadcasted_iota(jnp.int32, x.shape, 0)
    zero = jnp.zeros_like(x)
    return jnp.concatenate(
        [jnp.where(row < 64, x, zero), jnp.where(row < 64, zero, x)], axis=1
    )


def halves(x):
    lane = lax.broadcasted_iota(jnp.int32, x.shape, 1)
    zero = jnp.zeros_like(x)
    return jnp.concatenate(
        [jnp.where(lane < 64, x, zero), jnp.where(lane < 64, zero, x)], axis=0
    )


def diagonal(x):
    return jnp.concatenate([x[:64, :128], x[64:, 128:]], axis=0)


def kernel(
    q_hbm, k_hbm, v_hbm, g_hbm, w_hbm, pair_hbm, count_hbm,
    dq_hbm, dk_hbm, dv_hbm, wo_ref,
    kv, kvt, qs, gm, graw, gown, ww, do, pc, pcs,
    sbuf, pbuf, dsb, scale, att, acc, dqs,
    hold, back, got, hold2, fin, wsum, wgot, w2, w2got, w3, w3got,
    pair_ref, count_ref, loc, a_s, a_r, b_s, b_r, l_s, l_r, d_s, d_r, m_s, m_r, f_s, f_r, u_s, u_r, x_s, x_r, y_s, y_r,
):
    me = lax.axis_index("dz")
    p = lax.axis_index("dxy")
    low = me < 2
    sib = me + 1 - 2 * (me % 2)
    zpeer = (me + 2) % 4
    zdiag = (sib + 2) % 4
    group = (sib, zpeer, zdiag)
    places = 64

    def logical(layer, at):
        return jnp.where(at < 2, layer, 3 - layer)

    def layer_of(ll):
        return jnp.where(low, ll, 3 - ll)

    mine = logical(me, me)

    has = {DOWN: p > 0, UP: p < places - 1}
    gets = {DOWN: p < places - 1, UP: p > 0}
    step = {DOWN: -1, UP: 1}
    cross = {
        DOWN: (p % 16 == 0) & (p > 0),
        UP: (p % 16 == 15) & (p < places - 1),
    }
    crossed = {DOWN: (p % 16 == 15) & (p < places - 1), UP: (p % 16 == 0) & (p > 0)}
    relays = {}
    for r in (1, 2, 3):
        relays[UP, r] = (p % 16 == (15 + VIA[r]) % 16) & (p - VIA[r] < places - 1)
        relays[DOWN, r] = (p % 16 == -VIA[r] % 16) & (p + VIA[r] > 0)

    def via(d, r):
        return cl(p + step[d] * VIA[r])

    def relay_from(d, r):
        return cl(p - step[d] * VIA[r])

    def relay_to(d, r):
        return cl(p + step[d] * ONTO[r])

    def crossed_via(d, r):
        return cl(p - step[d] * ONTO[r])

    side = {DOWN: 2, UP: 0}

    def cl(x):
        return jnp.clip(x, 0, places - 1)

    def rows(ll, j):
        return pl.ds(pl.multiple_of((ll * 3 + j) * CELL, CELL), CELL)

    def cols(t):
        return pl.ds(pl.multiple_of(t * GW, GW), GW)

    def cell(ll):
        return pl.ds(pl.multiple_of(ll * CELL, CELL), CELL)

    def remote(src, dst, ss, rs, dz, place):
        return pltpu.make_async_remote_copy(
            src_ref=src, dst_ref=dst, send_sem=ss, recv_sem=rs,
            device_id=(dz, place), device_id_type=MESH,
        )

    own = cols(me)
    loads = [
        pltpu.make_async_copy(k_hbm.at[:, own], kv.at[0, rows(mine, 1)], loc.at[0]),
        pltpu.make_async_copy(v_hbm.at[:, own], kv.at[1, rows(mine, 1)], loc.at[1]),
        pltpu.make_async_copy(q_hbm.at[:, own], qs.at[cell(mine)], loc.at[2]),
        pltpu.make_async_copy(g_hbm, graw, loc.at[3]),
        pltpu.make_async_copy(w_hbm.at[:, own], ww, loc.at[4]),
    ]
    tables = [
        pltpu.make_async_copy(pair_hbm, pair_ref, loc.at[5]),
        pltpu.make_async_copy(count_hbm, count_ref, loc.at[6]),
    ]
    for c in tables + loads:
        c.start()

    zh, y, x = p // 16, (p // 4) % 4, p % 4
    at = zh * 4 + me

    def in_column(e):
        return zh * 16 + ((y + e) % 4) * 4 + x

    def in_row(e):
        return zh * 16 + y * 4 + (x + e) % 4

    def across(e):
        to = (at + e) % 16
        return to % 4, (to // 4) * 16 + y * 4 + x

    peers = []
    for e in range(1, 4):
        peers.append((None, me, in_column(e)))
        peers.append((None, me, in_row(e)))
    for e in range(1, 16):
        peers.append((None, *across(e)))
    for d in (DOWN, UP):
        peers.append((has[d], me, cl(p + step[d])))
        for r in (1, 2, 3):
            peers.append((cross[d], me, via(d, r)))
            peers.append((relays[d, r], me, relay_from(d, r)))
            peers.append((relays[d, r], me, relay_to(d, r)))
            peers.append((crossed[d], me, crossed_via(d, r)))
    barrier = pltpu.get_barrier_semaphore()
    expect = 0
    for ok, a, b in peers:

        def greet(a=a, b=b):
            pl.semaphore_signal(barrier, inc=1, device_id=(a, b), device_id_type=MESH)

        if ok is None:
            greet()
            expect = expect + 1
        else:
            pl.when(ok)(greet)
            expect = expect + jnp.where(ok, 1, 0)

    for c in tables:
        c.wait()
    lane = lax.broadcasted_iota(jnp.int32, (8, 128), 1)
    plain = jnp.zeros((8, 128), jnp.int32)
    turned = jnp.zeros((8, 128), jnp.int32)
    for s in range(9):
        plain = jnp.where(lane == s, pair_ref[0, s], plain)
        turned = jnp.where(lane == (2 - s // 3) * 3 + s % 3, pair_ref[0, s], turned)
    pcs[0] = plain
    pcs[1] = turned
    pc[mine] = jnp.where(low, plain, turned)

    def clear(d):
        for ll in range(4):
            kv[:, (ll * 3 + side[d]) * CELL : (ll * 3 + side[d] + 1) * CELL, :] = (
                jnp.zeros((2, CELL, GW), BF)
            )
            got[d, ll] = jnp.zeros((2, CELL, GW), BF)

    for d in (DOWN, UP):
        pl.when(jnp.logical_not(gets[d]))(lambda d=d: clear(d))

    pl.semaphore_wait(barrier, expect)

    def landing(kind, ll):
        if kind == C_:
            return pc.at[ll]
        if kind in (K_, V_):
            return kv.at[kind, rows(ll, 1)]
        return {Q_: qs, G_: gm}[kind].at[cell(ll)]

    def spread(kind, i):
        t = group[i]
        lt = logical(me, t)
        if kind == C_:
            src = pcs.at[jnp.where(t < 2, 0, 1)]
        elif kind == G_:
            src = gown
        else:
            src = {K_: k_hbm, V_: v_hbm, Q_: q_hbm}[kind].at[:, cols(t)]
        return remote(
            src, landing(kind, lt), a_s.at[kind, i], a_r.at[kind, lt], t, p
        )

    def arrived(kind, ll):
        dst = landing(kind, ll)
        remote(dst, dst, a_s.at[kind, 0], a_r.at[kind, ll], sib, p).wait_recv()

    for kind in (K_, V_, C_):
        for i in range(3):
            spread(kind, i).start()
    spread(Q_, 0).start()

    def halo(d, ll, kind):
        blk = kv.at[kind, rows(ll, 1)]
        dst = kv.at[kind, rows(ll, side[d])]
        return remote(
            blk, dst, b_s.at[d, ll, kind], b_r.at[d, ll, kind], me, cl(p + step[d])
        )

    def halo_detour(d, ll, kind, r):
        blk = kv.at[kind, rows(ll, 1)]
        return remote(
            blk, hold.at[d, ll], b_s.at[d, ll, kind], l_r.at[d, ll], me, via(d, r)
        )

    def halo_forward(d, ll, kind, r):
        dst = kv.at[kind, rows(ll, side[d])]
        return remote(
            hold.at[d, ll], dst, l_s.at[d, ll], b_r.at[d, ll, kind], me, relay_to(d, r)
        )

    def part(d, ll, kind):
        return remote(
            back.at[d, ll, kind], got.at[d, ll, kind],
            d_s.at[d, ll, kind], d_r.at[d, ll, kind], me, cl(p + step[d]),
        )

    def part_detour(d, ll, kind, r):
        return remote(
            back.at[d, ll, kind], hold2.at[d, ll],
            d_s.at[d, ll, kind], m_r.at[d, ll], me, via(d, r),
        )

    def part_forward(d, ll, kind, r):
        return remote(
            hold2.at[d, ll], got.at[d, ll, kind],
            m_s.at[d, ll], d_r.at[d, ll, kind], me, relay_to(d, r),
        )

    def send_beside(pos, ll, kind, straight, detour):
        r = WAY[pos, kind]
        for d in (UP, DOWN):
            if r == 0:
                pl.when(has[d])(lambda d=d: straight(d, ll, kind).start())
            else:
                pl.when(has[d] & jnp.logical_not(cross[d]))(
                    lambda d=d: straight(d, ll, kind).start()
                )
                pl.when(cross[d])(lambda d=d: detour(d, ll, kind, r).start())

    def pass_on(pos, ll, detour, forward):
        for kind in (0, 1):
            r = WAY[pos, kind]
            if r == 0:
                continue
            for d in (UP, DOWN):

                def go(d=d):
                    detour(d, ll, kind, r).wait_recv()
                    forward(d, ll, kind, r).start()

                pl.when(relays[d, r])(go)

    def send_halo(pos, ll, kind):
        send_beside(pos, ll, kind, halo, halo_detour)

    def forward_halo(pos, ll):
        pass_on(pos, ll, halo_detour, halo_forward)

    other = 1 - mine
    loads[0].wait()
    send_halo(0, mine, 0)
    loads[1].wait()
    send_halo(0, mine, 1)
    loads[3].wait()
    live = lax.broadcasted_iota(jnp.int32, (CELL, 1024), 0) < count_ref[0]
    gown[...] = jnp.where(live, graw[...], jnp.zeros((CELL, 1024), BF))
    own_g = pltpu.make_async_copy(gown, gm.at[cell(mine)], loc.at[5])
    own_g.start()
    spread(G_, 0).start()
    for kind in (0, 1):
        arrived(kind, other)
        send_halo(1, other, kind)
    forward_halo(0, mine)
    for kind in (0, 1):
        for ll in (2, 3):
            arrived(kind, ll)
            send_halo(ll, ll, kind)
        if kind == 0:
            spread(Q_, 1).start()
            spread(Q_, 2).start()
            forward_halo(1, other)
    spread(G_, 1).start()
    zl = logical(zpeer, me)
    g_fwd = remote(
        gm.at[cell(zl)], gm.at[cell(zl)], a_s.at[G_, 2], a_r.at[G_, zl], sib, p
    )

    def halo_arrived(ll):
        for d in (UP, DOWN):
            for kind in (0, 1):
                pl.when(gets[d])(lambda d=d, kind=kind: halo(d, ll, kind).wait_recv())

    def turn_layer(ll):
        for j in range(3):
            for kind in (0, 1):
                at_ = (ll * 3 + j) * CELL
                kvt[kind, :, at_ : at_ + CELL] = kv[kind, at_ : at_ + CELL, :].T

    first = [0, 0, 1, 2]
    last = [1, 2, 3, 3]
    base = [0, 768, 1920, 3072]
    sub = lax.broadcasted_iota(jnp.int32, (CELL, 128), 0)

    def fold(op, v):
        return op(v.reshape(CELL // 8, 8, 256), axis=0)

    def forward(lq):
        bias = jnp.where(sub < pc[lq][0:1, :], 0.0, NEG)
        slots = [(ll, j) for ll in range(first[lq], last[lq] + 1) for j in range(3)]
        n = len(slots) * CELL
        r0 = first[lq] * 3 * CELL
        cq = slice(lq * CELL, (lq + 1) * CELL)
        for hp in range(2):
            hc = slice(hp * 128, hp * 128 + 128)
            qt = halves_t((qs[cq, hc] * jnp.asarray(0.125, BF)).T)
            top = None
            for i, (ll, j) in enumerate(slots):
                at_ = (ll * 3 + j) * CELL
                k9 = (ll - lq + 1) * 3 + j
                s = dot(kv[0, at_ : at_ + CELL, hc], qt) + bias[:, k9 : k9 + 1]
                sbuf[i * CELL : (i + 1) * CELL, :] = s
                t = fold(jnp.max, s)
                top = t if top is None else jnp.maximum(top, t)
            top = jnp.max(top, axis=0, keepdims=True)
            total = None
            b0 = base[lq]
            for i in range(len(slots)):
                e = jnp.exp(sbuf[i * CELL : (i + 1) * CELL, :] - top)
                pbuf[hp, b0 + i * CELL : b0 + (i + 1) * CELL, :] = e.astype(BF)
                t = fold(jnp.sum, e)
                total = t if total is None else total + t
            inv = 1.0 / jnp.sum(total, axis=0, keepdims=True)
            at_t = dot(kvt[1, hc, r0 : r0 + n], pbuf[hp, b0 : b0 + n, :])
            att[hc, cq] = diagonal(at_t * inv).astype(BF)
            scale[lq, hp] = jnp.broadcast_to(inv, (8, 256))

    def backward(lq):
        slots = [(ll, j) for ll in range(first[lq], last[lq] + 1) for j in range(3)]
        n = len(slots) * CELL
        r0 = first[lq] * 3 * CELL
        cq = slice(lq * CELL, (lq + 1) * CELL)
        b0 = base[lq]
        for hp in range(2):
            hc = slice(hp * 128, hp * 128 + 128)
            inv = scale[lq, hp][0:1, :]
            inv = jnp.concatenate(
                [
                    jnp.broadcast_to(inv[:, :128], (64, 128)),
                    jnp.broadcast_to(inv[:, 128:], (64, 128)),
                ],
                axis=0,
            )
            dt = (do[cq, hc].T.astype(F32) * inv).astype(BF)
            prod = dt.astype(F32) * att[hc, cq].astype(F32)
            dl = jnp.concatenate(
                [
                    jnp.sum(prod[:64], axis=0, keepdims=True),
                    jnp.sum(prod[64:], axis=0, keepdims=True),
                ],
                axis=1,
            )
            dmt = halves_t(dt)
            dm = halves(dt.T)
            qm = halves(qs[cq, hc] * jnp.asarray(0.125, BF))
            for i, (ll, j) in enumerate(slots):
                at_ = (ll * 3 + j) * CELL
                pr = pbuf[hp, b0 + i * CELL : b0 + (i + 1) * CELL, :]
                dp = dot(kv[1, at_ : at_ + CELL, hc], dmt)
                ds = (pr.astype(F32) * (dp - dl)).astype(BF)
                dsb[i * CELL : (i + 1) * CELL, :] = ds
                dv = dot(pr, dm)
                dk = dot(ds, qm)
                if lq == max(ll - 1, 0):
                    acc[1, at_ : at_ + CELL, hc] = dv
                    acc[0, at_ : at_ + CELL, hc] = dk
                else:
                    acc[1, at_ : at_ + CELL, hc] += dv
                    acc[0, at_ : at_ + CELL, hc] += dk
            dqt = dot(kvt[0, hc, r0 : r0 + n], dsb[0:n, :])
            dqs[cq, hc] = (diagonal(dqt) * 0.125).T.astype(BF)

    def send_parts(ll):
        for d in (UP, DOWN):
            j = 2 if d == UP else 0
            at_ = (ll * 3 + j) * CELL
            for kind in (1, 0):
                back[d, ll, kind] = acc[kind, at_ : at_ + CELL, :].astype(BF)
        for kind in (1, 0):
            send_beside(ll, ll, kind, part, part_detour)

    def forward_parts(ll):
        pass_on(ll, ll, part_detour, part_forward)

    def home(kind, ll, src):
        t = layer_of(ll)
        out = (dk_hbm, dv_hbm, dq_hbm)[kind].at[:, cols(me)]
        o = (t - me + 4) % 4
        return remote(src, out, f_s.at[kind, ll], f_r.at[kind, o], t, p)

    def keep(kind, ll, src):
        out = (dk_hbm, dv_hbm, dq_hbm)[kind].at[:, cols(me)]
        return pltpu.make_async_copy(src, out, f_s.at[kind, ll])

    def send_home(kind, ll, src):
        if ll >= 2:
            home(kind, ll, src).start()
        else:
            pl.when(mine != ll)(lambda: home(kind, ll, src).start())
            pl.when(mine == ll)(lambda: keep(kind, ll, src).start())

    def sent_home(kind, ll, src):
        if ll >= 2:
            home(kind, ll, src).wait_send()
        else:
            pl.when(mine != ll)(lambda: home(kind, ll, src).wait_send())
            pl.when(mine == ll)(lambda: keep(kind, ll, src).wait())

    def finish(ll):
        for d in (UP, DOWN):
            for kind in (0, 1):
                pl.when(gets[d])(lambda d=d, kind=kind: part(d, ll, kind).wait_recv())
        at_ = (ll * 3 + 1) * CELL
        for kind in (0, 1):
            s = acc[kind, at_ : at_ + CELL, :]
            s = s + got[0, ll, kind].astype(F32) + got[1, ll, kind].astype(F32)
            fin[kind, ll] = s.astype(BF)
            send_home(kind, ll, fin.at[kind, ll])

    left, right = pl.ds(0, 128), pl.ds(128, 128)

    def stage1(e):
        return (
            remote(
                wsum.at[:, (y + e) % 4, :, :, left], wgot.at[0, e],
                u_s.at[0, e], u_r.at[0, e], me, in_column(e),
            ),
            remote(
                wsum.at[:, :, (x + e) % 4, :, right], wgot.at[1, e],
                u_s.at[1, e], u_r.at[1, e], me, in_row(e),
            ),
        )

    def stage2(e):
        return (
            remote(
                w2.at[0, :, (x + e) % 4], w2got.at[0, e],
                y_s.at[0, e], y_r.at[0, e], me, in_row(e),
            ),
            remote(
                w2.at[1, :, (y + e) % 4], w2got.at[1, e],
                y_s.at[1, e], y_r.at[1, e], me, in_column(e),
            ),
        )

    def stage3(e):
        t, place = across(e)
        to = (at + e) % 16
        return remote(
            w3.at[to // 4], w3got.at[zh, :, cols(me)], x_s.at[e], x_r.at[e], t, place
        )

    loads[2].wait()
    loads[4].wait()
    own_g.wait()
    for kind in (C_, Q_, G_):
        arrived(kind, other)
    do[0 : 2 * CELL] = dot(gm[0 : 2 * CELL], ww[...]).astype(BF)
    forward_halo(3, 3)
    forward_halo(2, 2)
    halo_arrived(0)
    turn_layer(0)
    halo_arrived(1)
    turn_layer(1)
    forward(0)
    backward(0)
    send_home(2, 0, dqs.at[cell(0)])
    halo_arrived(2)
    turn_layer(2)
    forward(1)
    backward(1)
    send_parts(0)
    send_home(2, 1, dqs.at[cell(1)])
    for kind in (C_, Q_):
        arrived(kind, 2)
        arrived(kind, 3)
    halo_arrived(3)
    turn_layer(3)
    forward(2)
    forward(3)
    arrived(G_, zl)
    g_fwd.start()
    forward_parts(0)
    arrived(G_, 5 - zl)
    for i in range(4):
        w_t = dot(att[...], gm[:, i * 256 : (i + 1) * 256]).astype(BF)
        wsum[i] = w_t.T.reshape(4, 4, 16, GW)
    for e in range(1, 4):
        for c in stage1(e):
            c.start()
    do[2 * CELL : 4 * CELL] = dot(gm[2 * CELL : 4 * CELL], ww[...]).astype(BF)
    backward(2)
    send_parts(1)
    send_home(2, 2, dqs.at[cell(2)])
    backward(3)
    send_parts(3)
    send_parts(2)
    send_home(2, 3, dqs.at[cell(3)])

    s_l = wsum[:, y, :, :, 0:128].astype(F32)
    s_r = wsum[:, :, x, :, 128:256].astype(F32)
    for e in range(1, 4):
        for c in stage1(e):
            c.wait_recv()
        s_l = s_l + wgot[0, e].astype(F32)
        s_r = s_r + wgot[1, e].astype(F32)
    w2[0] = s_l.astype(BF)
    w2[1] = s_r.astype(BF)
    for e in range(1, 4):
        for c in stage2(e):
            c.start()
    finish(0)
    forward_parts(1)

    s_l = w2[0, :, x].astype(F32)
    s_r = w2[1, :, y].astype(F32)
    for e in range(1, 4):
        for c in stage2(e):
            c.wait_recv()
        s_l = s_l + w2got[0, e].astype(F32)
        s_r = s_r + w2got[1, e].astype(F32)
    w3[:, :, 0:128] = s_l.astype(BF)
    w3[:, :, 128:256] = s_r.astype(BF)
    for e in range(1, 16):
        stage3(e).start()
    own_x = pltpu.make_async_copy(w3.at[zh], w3got.at[zh, :, cols(me)], loc.at[7])
    own_x.start()
    finish(1)
    forward_parts(3)
    forward_parts(2)
    finish(3)
    finish(2)
    own_x.wait()
    for e in range(1, 16):
        came = (at - e + 16) % 16
        spot = w3got.at[came // 4, :, cols(came % 4)]
        remote(spot, spot, x_s.at[e], x_r.at[e], sib, p).wait_recv()
    total = w3got[0].astype(F32)
    for i in range(1, 4):
        total = total + w3got[i].astype(F32)
    wo_ref[...] = total * (32768**-0.5)

    for kind in range(3):
        for o in range(1, 4):
            spot = (dk_hbm, dv_hbm, dq_hbm)[kind].at[:, cols((me - o + 4) % 4)]
            remote(spot, spot, f_s.at[kind, 0], f_r.at[kind, o], sib, p).wait_recv()
    for ll in range(4):
        sent_home(0, ll, fin.at[0, ll])
        sent_home(1, ll, fin.at[1, ll])
        sent_home(2, ll, dqs.at[cell(ll)])
    for kind in (K_, V_, Q_, C_):
        for i in range(3):
            spread(kind, i).wait_send()
    spread(G_, 0).wait_send()
    spread(G_, 1).wait_send()
    g_fwd.wait_send()
    for e in range(1, 4):
        for c in stage1(e) + stage2(e):
            c.wait_send()
    for e in range(1, 16):
        stage3(e).wait_send()
    for d in (UP, DOWN):

        def sent(d=d):
            for ll in range(4):
                for kind in (0, 1):
                    halo(d, ll, kind).wait_send()
                    part(d, ll, kind).wait_send()

        pl.when(has[d])(sent)
        for pos, ll in enumerate((mine, other, 2, 3)):
            for kind in (0, 1):
                r = WAY[pos, kind]
                if r:
                    pl.when(relays[d, r])(
                        lambda d=d: halo_forward(d, ll, kind, r).wait_send()
                    )
                r = WAY[pos, kind]
                if r:
                    pl.when(relays[d, r])(
                        lambda d=d: part_forward(d, pos, kind, r).wait_send()
                    )


def shards(queries, keys, values, out_grad, out_weight, pair_counts, counts):
    n, width = queries.shape
    big = pl.BlockSpec(memory_space=pltpu.HBM)
    dma = pltpu.SemaphoreType.DMA
    wide = jax.ShapeDtypeStruct((n, width), BF)
    return pl.pallas_call(
        kernel,
        name="cell_attention_backward",
        out_shape=(wide, wide, wide, jax.ShapeDtypeStruct((16, width), F32)),
        in_specs=[big] * 7,
        out_specs=(big, big, big, pl.BlockSpec(memory_space=pltpu.VMEM)),
        scratch_shapes=[
            pltpu.VMEM((2, 1536, GW), BF),
            pltpu.VMEM((2, GW, 1536), BF),
            pltpu.VMEM((512, GW), BF),
            pltpu.VMEM((512, 1024), BF),
            pltpu.VMEM((CELL, 1024), BF),
            pltpu.VMEM((CELL, 1024), BF),
            pltpu.VMEM((1024, GW), BF),
            pltpu.VMEM((512, GW), BF),
            pltpu.VMEM((4, 8, 128), jnp.int32),
            pltpu.VMEM((2, 8, 128), jnp.int32),
            pltpu.VMEM((1152, 256), F32),
            pltpu.VMEM((2, 3840, 256), BF),
            pltpu.VMEM((1152, 256), BF),
            pltpu.VMEM((4, 2, 8, 256), F32),
            pltpu.VMEM((GW, 512), BF),
            pltpu.VMEM((2, 1536, GW), F32),
            pltpu.VMEM((512, GW), BF),
            pltpu.VMEM((2, 4, CELL, GW), BF),
            pltpu.VMEM((2, 4, 2, CELL, GW), BF),
            pltpu.VMEM((2, 4, 2, CELL, GW), BF),
            pltpu.VMEM((2, 4, CELL, GW), BF),
            pltpu.VMEM((2, 4, CELL, GW), BF),
            pltpu.VMEM((4, 4, 4, 16, GW), BF),
            pltpu.VMEM((2, 4, 4, 4, 16, 128), BF),
            pltpu.VMEM((2, 4, 4, 16, 128), BF),
            pltpu.VMEM((2, 4, 4, 16, 128), BF),
            pltpu.VMEM((4, 16, GW), BF),
            pltpu.VMEM((4, 16, 1024), BF),
            pltpu.SMEM((1, 9), jnp.int32),
            pltpu.SMEM((1,), jnp.int32),
            dma((8,)),
            dma((5, 4)),
            dma((5, 4)),
            dma((2, 4, 2)),
            dma((2, 4, 2)),
            dma((2, 4)),
            dma((2, 4)),
            dma((2, 4, 2)),
            dma((2, 4, 2)),
            dma((2, 4)),
            dma((2, 4)),
            dma((3, 4)),
            dma((3, 4)),
            dma((2, 4)),
            dma((2, 4)),
            dma((16,)),
            dma((16,)),
            dma((2, 4)),
            dma((2, 4)),
        ],
        compiler_params=pltpu.CompilerParams(
            collective_id=0, has_side_effects=True, vmem_limit_bytes=53 * 2**20
        ),
        cost_estimate=pl.CostEstimate(
            flops=3_000_000_000, bytes_accessed=4_000_000, transcendentals=2_000_000
        ),
    )(queries, keys, values, out_grad, out_weight, pair_counts, counts)


def solution(mesh):
    both = P(("dz", "dxy"), None)
    return jax.shard_map(
        shards,
        mesh=mesh,
        in_specs=(both, both, both, both, P(), both, P(("dz", "dxy"))),
        out_specs=(both, both, both, P("dxy", None)),
        check_vma=False,
    )
```

```python
import jax
import jax.numpy as jnp
from jax import lax
from jax.experimental import pallas as pl
from jax.experimental.pallas import tpu as pltpu
from jax.sharding import PartitionSpec as P

MESH = pl.DeviceIdType.MESH
BF = jnp.bfloat16
F32 = jnp.float32
CELL = 128
GW = 256
DOWN, UP = 0, 1
K_, V_, Q_, G_, C_ = 0, 1, 2, 3, 4
WAY = {(0, 0): 1, (0, 1): 2, (1, 0): 3, (1, 1): 0, (2, 0): 1, (2, 1): 2, (3, 0): 3, (3, 1): 0}
VIA = {1: -15, 2: -3, 3: -12}
ONTO = {1: 16, 2: 4, 3: 13}
NEG = -1e30


def dot(a, b):
    return jnp.dot(a, b, preferred_element_type=F32)


def halves_t(x):
    row = lax.broadcasted_iota(jnp.int32, x.shape, 0)
    zero = jnp.zeros_like(x)
    return jnp.concatenate(
        [jnp.where(row < 64, x, zero), jnp.where(row < 64, zero, x)], axis=1
    )


def halves(x):
    lane = lax.broadcasted_iota(jnp.int32, x.shape, 1)
    zero = jnp.zeros_like(x)
    return jnp.concatenate(
        [jnp.where(lane < 64, x, zero), jnp.where(lane < 64, zero, x)], axis=0
    )


def diagonal(x):
    return jnp.concatenate([x[:64, :128], x[64:, 128:]], axis=0)


def kernel(
    q_hbm, k_hbm, v_hbm, g_hbm, w_hbm, pair_hbm, count_hbm,
    dq_hbm, dk_hbm, dv_hbm, wo_ref,
    kv, kvt, qs, gm, graw, gown, ww, do, pc, pcs,
    sbuf, pbuf, dsb, scale, att, acc, dqs,
    hold, back, got, hold2, fin, wsum, wgot, w2, w2got, w3, w3got,
    pair_ref, count_ref, loc, a_s, a_r, b_s, b_r, l_s, l_r, d_s, d_r, m_s, m_r, f_s, f_r, u_s, u_r, x_s, x_r, y_s, y_r,
):
    me = lax.axis_index("dz")
    p = lax.axis_index("dxy")
    low = me < 2
    sib = me + 1 - 2 * (me % 2)
    zpeer = (me + 2) % 4
    zdiag = (sib + 2) % 4
    group = (sib, zpeer, zdiag)
    places = 64

    def logical(layer, at):
        return jnp.where(at < 2, layer, 3 - layer)

    def layer_of(ll):
        return jnp.where(low, ll, 3 - ll)

    mine = logical(me, me)

    has = {DOWN: p > 0, UP: p < places - 1}
    gets = {DOWN: p < places - 1, UP: p > 0}
    step = {DOWN: -1, UP: 1}
    cross = {
        DOWN: (p % 16 == 0) & (p > 0),
        UP: (p % 16 == 15) & (p < places - 1),
    }
    crossed = {DOWN: (p % 16 == 15) & (p < places - 1), UP: (p % 16 == 0) & (p > 0)}
    relays = {}
    for r in (1, 2, 3):
        relays[UP, r] = (p % 16 == (15 + VIA[r]) % 16) & (p - VIA[r] < places - 1)
        relays[DOWN, r] = (p % 16 == -VIA[r] % 16) & (p + VIA[r] > 0)

    def via(d, r):
        return cl(p + step[d] * VIA[r])

    def relay_from(d, r):
        return cl(p - step[d] * VIA[r])

    def relay_to(d, r):
        return cl(p + step[d] * ONTO[r])

    def crossed_via(d, r):
        return cl(p - step[d] * ONTO[r])

    side = {DOWN: 2, UP: 0}

    def cl(x):
        return jnp.clip(x, 0, places - 1)

    def rows(ll, j):
        return pl.ds(pl.multiple_of((ll * 3 + j) * CELL, CELL), CELL)

    def cols(t):
        return pl.ds(pl.multiple_of(t * GW, GW), GW)

    def cell(ll):
        return pl.ds(pl.multiple_of(ll * CELL, CELL), CELL)

    def remote(src, dst, ss, rs, dz, place):
        return pltpu.make_async_remote_copy(
            src_ref=src, dst_ref=dst, send_sem=ss, recv_sem=rs,
            device_id=(dz, place), device_id_type=MESH,
        )

    own = cols(me)
    loads = [
        pltpu.make_async_copy(k_hbm.at[:, own], kv.at[0, rows(mine, 1)], loc.at[0]),
        pltpu.make_async_copy(v_hbm.at[:, own], kv.at[1, rows(mine, 1)], loc.at[1]),
        pltpu.make_async_copy(q_hbm.at[:, own], qs.at[cell(mine)], loc.at[2]),
        pltpu.make_async_copy(g_hbm, graw, loc.at[3]),
        pltpu.make_async_copy(w_hbm.at[:, own], ww, loc.at[4]),
    ]
    tables = [
        pltpu.make_async_copy(pair_hbm, pair_ref, loc.at[5]),
        pltpu.make_async_copy(count_hbm, count_ref, loc.at[6]),
    ]
    for c in tables + loads:
        c.start()

    zh, y, x = p // 16, (p // 4) % 4, p % 4
    at = zh * 4 + me

    def in_column(e):
        return zh * 16 + ((y + e) % 4) * 4 + x

    def in_row(e):
        return zh * 16 + y * 4 + (x + e) % 4

    def across(e):
        to = (at + e) % 16
        return to % 4, (to // 4) * 16 + y * 4 + x

    peers = []
    for e in range(1, 4):
        peers.append((None, me, in_column(e)))
        peers.append((None, me, in_row(e)))
    for e in range(1, 16):
        peers.append((None, *across(e)))
    for d in (DOWN, UP):
        peers.append((has[d], me, cl(p + step[d])))
        for r in (1, 2, 3):
            peers.append((cross[d], me, via(d, r)))
            peers.append((relays[d, r], me, relay_from(d, r)))
            peers.append((relays[d, r], me, relay_to(d, r)))
            peers.append((crossed[d], me, crossed_via(d, r)))
    barrier = pltpu.get_barrier_semaphore()
    expect = 0
    for ok, a, b in peers:

        def greet(a=a, b=b):
            pl.semaphore_signal(barrier, inc=1, device_id=(a, b), device_id_type=MESH)

        if ok is None:
            greet()
            expect = expect + 1
        else:
            pl.when(ok)(greet)
            expect = expect + jnp.where(ok, 1, 0)

    for c in tables:
        c.wait()
    lane = lax.broadcasted_iota(jnp.int32, (8, 128), 1)
    plain = jnp.zeros((8, 128), jnp.int32)
    turned = jnp.zeros((8, 128), jnp.int32)
    for s in range(9):
        plain = jnp.where(lane == s, pair_ref[0, s], plain)
        turned = jnp.where(lane == (2 - s // 3) * 3 + s % 3, pair_ref[0, s], turned)
    pcs[0] = plain
    pcs[1] = turned
    pc[mine] = jnp.where(low, plain, turned)

    def clear(d):
        for ll in range(4):
            kv[:, (ll * 3 + side[d]) * CELL : (ll * 3 + side[d] + 1) * CELL, :] = (
                jnp.zeros((2, CELL, GW), BF)
            )
            got[d, ll] = jnp.zeros((2, CELL, GW), BF)

    for d in (DOWN, UP):
        pl.when(jnp.logical_not(gets[d]))(lambda d=d: clear(d))

    pl.semaphore_wait(barrier, expect)

    def landing(kind, ll):
        if kind == C_:
            return pc.at[ll]
        if kind in (K_, V_):
            return kv.at[kind, rows(ll, 1)]
        return {Q_: qs, G_: gm}[kind].at[cell(ll)]

    def spread(kind, i):
        t = group[i]
        lt = logical(me, t)
        if kind == C_:
            src = pcs.at[jnp.where(t < 2, 0, 1)]
        elif kind == G_:
            src = gown
        else:
            src = {K_: k_hbm, V_: v_hbm, Q_: q_hbm}[kind].at[:, cols(t)]
        return remote(
            src, landing(kind, lt), a_s.at[kind, i], a_r.at[kind, lt], t, p
        )

    def arrived(kind, ll):
        dst = landing(kind, ll)
        remote(dst, dst, a_s.at[kind, 0], a_r.at[kind, ll], sib, p).wait_recv()

    for kind in (K_, V_, C_):
        for i in range(3):
            spread(kind, i).start()
    spread(Q_, 0).start()

    def halo(d, ll, kind):
        blk = kv.at[kind, rows(ll, 1)]
        dst = kv.at[kind, rows(ll, side[d])]
        return remote(
            blk, dst, b_s.at[d, ll, kind], b_r.at[d, ll, kind], me, cl(p + step[d])
        )

    def halo_detour(d, ll, kind, r):
        blk = kv.at[kind, rows(ll, 1)]
        return remote(
            blk, hold.at[d, ll], b_s.at[d, ll, kind], l_r.at[d, ll], me, via(d, r)
        )

    def halo_forward(d, ll, kind, r):
        dst = kv.at[kind, rows(ll, side[d])]
        return remote(
            hold.at[d, ll], dst, l_s.at[d, ll], b_r.at[d, ll, kind], me, relay_to(d, r)
        )

    def part(d, ll, kind):
        return remote(
            back.at[d, ll, kind], got.at[d, ll, kind],
            d_s.at[d, ll, kind], d_r.at[d, ll, kind], me, cl(p + step[d]),
        )

    def part_detour(d, ll, kind, r):
        return remote(
            back.at[d, ll, kind], hold2.at[d, ll],
            d_s.at[d, ll, kind], m_r.at[d, ll], me, via(d, r),
        )

    def part_forward(d, ll, kind, r):
        return remote(
            hold2.at[d, ll], got.at[d, ll, kind],
            m_s.at[d, ll], d_r.at[d, ll, kind], me, relay_to(d, r),
        )

    def send_beside(pos, ll, kind, straight, detour):
        r = WAY[pos, kind]
        for d in (UP, DOWN):
            if r == 0:
                pl.when(has[d])(lambda d=d: straight(d, ll, kind).start())
            else:
                pl.when(has[d] & jnp.logical_not(cross[d]))(
                    lambda d=d: straight(d, ll, kind).start()
                )
                pl.when(cross[d])(lambda d=d: detour(d, ll, kind, r).start())

    def pass_on(pos, ll, detour, forward):
        for kind in (0, 1):
            r = WAY[pos, kind]
            if r == 0:
                continue
            for d in (UP, DOWN):

                def go(d=d):
                    detour(d, ll, kind, r).wait_recv()
                    forward(d, ll, kind, r).start()

                pl.when(relays[d, r])(go)

    def send_halo(pos, ll, kind):
        send_beside(pos, ll, kind, halo, halo_detour)

    def forward_halo(pos, ll):
        pass_on(pos, ll, halo_detour, halo_forward)

    other = 1 - mine
    loads[0].wait()
    send_halo(0, mine, 0)
    loads[1].wait()
    send_halo(0, mine, 1)
    loads[3].wait()
    live = lax.broadcasted_iota(jnp.int32, (CELL, 1024), 0) < count_ref[0]
    gown[...] = jnp.where(live, graw[...], jnp.zeros((CELL, 1024), BF))
    own_g = pltpu.make_async_copy(gown, gm.at[cell(mine)], loc.at[5])
    own_g.start()
    spread(G_, 0).start()
    for kind in (0, 1):
        arrived(kind, other)
        send_halo(1, other, kind)
    forward_halo(0, mine)
    for kind in (0, 1):
        for ll in (2, 3):
            arrived(kind, ll)
            send_halo(ll, ll, kind)
        if kind == 0:
            spread(Q_, 1).start()
            spread(Q_, 2).start()
            forward_halo(1, other)
    spread(G_, 1).start()
    zl = logical(zpeer, me)
    g_fwd = remote(
        gm.at[cell(zl)], gm.at[cell(zl)], a_s.at[G_, 2], a_r.at[G_, zl], sib, p
    )

    def halo_arrived(ll):
        for d in (UP, DOWN):
            for kind in (0, 1):
                pl.when(gets[d])(lambda d=d, kind=kind: halo(d, ll, kind).wait_recv())

    def turn_layer(ll):
        for j in range(3):
            for kind in (0, 1):
                at_ = (ll * 3 + j) * CELL
                kvt[kind, :, at_ : at_ + CELL] = kv[kind, at_ : at_ + CELL, :].T

    first = [0, 0, 1, 2]
    last = [1, 2, 3, 3]
    base = [0, 768, 1920, 3072]
    sub = lax.broadcasted_iota(jnp.int32, (CELL, 128), 0)

    def fold(op, v):
        return op(v.reshape(CELL // 8, 8, 256), axis=0)

    def forward(lq):
        bias = jnp.where(sub < pc[lq][0:1, :], 0.0, NEG)
        slots = [(ll, j) for ll in range(first[lq], last[lq] + 1) for j in range(3)]
        n = len(slots) * CELL
        r0 = first[lq] * 3 * CELL
        cq = slice(lq * CELL, (lq + 1) * CELL)
        for hp in range(2):
            hc = slice(hp * 128, hp * 128 + 128)
            qt = halves_t((qs[cq, hc] * jnp.asarray(0.125, BF)).T)
            top = None
            for i, (ll, j) in enumerate(slots):
                at_ = (ll * 3 + j) * CELL
                k9 = (ll - lq + 1) * 3 + j
                s = dot(kv[0, at_ : at_ + CELL, hc], qt) + bias[:, k9 : k9 + 1]
                sbuf[i * CELL : (i + 1) * CELL, :] = s
                t = fold(jnp.max, s)
                top = t if top is None else jnp.maximum(top, t)
            top = jnp.max(top, axis=0, keepdims=True)
            total = None
            b0 = base[lq]
            for i in range(len(slots)):
                e = jnp.exp(sbuf[i * CELL : (i + 1) * CELL, :] - top)
                pbuf[hp, b0 + i * CELL : b0 + (i + 1) * CELL, :] = e.astype(BF)
                t = fold(jnp.sum, e)
                total = t if total is None else total + t
            inv = 1.0 / jnp.sum(total, axis=0, keepdims=True)
            at_t = dot(kvt[1, hc, r0 : r0 + n], pbuf[hp, b0 : b0 + n, :])
            att[hc, cq] = diagonal(at_t * inv).astype(BF)
            scale[lq, hp] = jnp.broadcast_to(inv, (8, 256))

    def backward(lq):
        slots = [(ll, j) for ll in range(first[lq], last[lq] + 1) for j in range(3)]
        n = len(slots) * CELL
        r0 = first[lq] * 3 * CELL
        cq = slice(lq * CELL, (lq + 1) * CELL)
        b0 = base[lq]
        for hp in range(2):
            hc = slice(hp * 128, hp * 128 + 128)
            inv = scale[lq, hp][0:1, :]
            inv = jnp.concatenate(
                [
                    jnp.broadcast_to(inv[:, :128], (64, 128)),
                    jnp.broadcast_to(inv[:, 128:], (64, 128)),
                ],
                axis=0,
            )
            dt = (do[cq, hc].T.astype(F32) * inv).astype(BF)
            prod = dt.astype(F32) * att[hc, cq].astype(F32)
            dl = jnp.concatenate(
                [
                    jnp.sum(prod[:64], axis=0, keepdims=True),
                    jnp.sum(prod[64:], axis=0, keepdims=True),
                ],
                axis=1,
            )
            dmt = halves_t(dt)
            dm = halves(dt.T)
            qm = halves(qs[cq, hc] * jnp.asarray(0.125, BF))
            for i, (ll, j) in enumerate(slots):
                at_ = (ll * 3 + j) * CELL
                pr = pbuf[hp, b0 + i * CELL : b0 + (i + 1) * CELL, :]
                dp = dot(kv[1, at_ : at_ + CELL, hc], dmt)
                ds = (pr.astype(F32) * (dp - dl)).astype(BF)
                dsb[i * CELL : (i + 1) * CELL, :] = ds
                dv = dot(pr, dm)
                dk = dot(ds, qm)
                if lq == max(ll - 1, 0):
                    acc[1, at_ : at_ + CELL, hc] = dv
                    acc[0, at_ : at_ + CELL, hc] = dk
                else:
                    acc[1, at_ : at_ + CELL, hc] += dv
                    acc[0, at_ : at_ + CELL, hc] += dk
            dqt = dot(kvt[0, hc, r0 : r0 + n], dsb[0:n, :])
            dqs[cq, hc] = (diagonal(dqt) * 0.125).T.astype(BF)

    def send_parts(ll):
        for d in (UP, DOWN):
            j = 2 if d == UP else 0
            at_ = (ll * 3 + j) * CELL
            for kind in (1, 0):
                back[d, ll, kind] = acc[kind, at_ : at_ + CELL, :].astype(BF)
        for kind in (1, 0):
            send_beside(ll, ll, kind, part, part_detour)

    def forward_parts(ll):
        pass_on(ll, ll, part_detour, part_forward)

    def home(kind, ll, src):
        t = layer_of(ll)
        out = (dk_hbm, dv_hbm, dq_hbm)[kind].at[:, cols(me)]
        o = (t - me + 4) % 4
        return remote(src, out, f_s.at[kind, ll], f_r.at[kind, o], t, p)

    def keep(kind, ll, src):
        out = (dk_hbm, dv_hbm, dq_hbm)[kind].at[:, cols(me)]
        return pltpu.make_async_copy(src, out, f_s.at[kind, ll])

    def send_home(kind, ll, src):
        if ll >= 2:
            home(kind, ll, src).start()
        else:
            pl.when(mine != ll)(lambda: home(kind, ll, src).start())
            pl.when(mine == ll)(lambda: keep(kind, ll, src).start())

    def sent_home(kind, ll, src):
        if ll >= 2:
            home(kind, ll, src).wait_send()
        else:
            pl.when(mine != ll)(lambda: home(kind, ll, src).wait_send())
            pl.when(mine == ll)(lambda: keep(kind, ll, src).wait())

    def finish(ll):
        for d in (UP, DOWN):
            for kind in (0, 1):
                pl.when(gets[d])(lambda d=d, kind=kind: part(d, ll, kind).wait_recv())
        at_ = (ll * 3 + 1) * CELL
        for kind in (0, 1):
            s = acc[kind, at_ : at_ + CELL, :]
            s = s + got[0, ll, kind].astype(F32) + got[1, ll, kind].astype(F32)
            fin[kind, ll] = s.astype(BF)
            send_home(kind, ll, fin.at[kind, ll])

    left, right = pl.ds(0, 128), pl.ds(128, 128)

    def stage1(e):
        return (
            remote(
                wsum.at[:, (y + e) % 4, :, :, left], wgot.at[0, e],
                u_s.at[0, e], u_r.at[0, e], me, in_column(e),
            ),
            remote(
                wsum.at[:, :, (x + e) % 4, :, right], wgot.at[1, e],
                u_s.at[1, e], u_r.at[1, e], me, in_row(e),
            ),
        )

    def stage2(e):
        return (
            remote(
                w2.at[0, :, (x + e) % 4], w2got.at[0, e],
                y_s.at[0, e], y_r.at[0, e], me, in_row(e),
            ),
            remote(
                w2.at[1, :, (y + e) % 4], w2got.at[1, e],
                y_s.at[1, e], y_r.at[1, e], me, in_column(e),
            ),
        )

    def stage3(e):
        t, place = across(e)
        to = (at + e) % 16
        return remote(
            w3.at[to // 4], w3got.at[zh, :, cols(me)], x_s.at[e], x_r.at[e], t, place
        )

    loads[2].wait()
    loads[4].wait()
    own_g.wait()
    for kind in (C_, Q_, G_):
        arrived(kind, other)
    do[0 : 2 * CELL] = dot(gm[0 : 2 * CELL], ww[...]).astype(BF)
    forward_halo(3, 3)
    forward_halo(2, 2)
    halo_arrived(0)
    turn_layer(0)
    halo_arrived(1)
    turn_layer(1)
    forward(0)
    backward(0)
    send_home(2, 0, dqs.at[cell(0)])
    halo_arrived(2)
    turn_layer(2)
    forward(1)
    backward(1)
    send_parts(0)
    send_home(2, 1, dqs.at[cell(1)])
    for kind in (C_, Q_):
        arrived(kind, 2)
        arrived(kind, 3)
    halo_arrived(3)
    turn_layer(3)
    forward(2)
    forward(3)
    arrived(G_, zl)
    g_fwd.start()
    forward_parts(0)
    arrived(G_, 5 - zl)
    for i in range(4):
        w_t = dot(att[...], gm[:, i * 256 : (i + 1) * 256]).astype(BF)
        wsum[i] = w_t.T.reshape(4, 4, 16, GW)
    for e in range(1, 4):
        for c in stage1(e):
            c.start()
    do[2 * CELL : 4 * CELL] = dot(gm[2 * CELL : 4 * CELL], ww[...]).astype(BF)
    backward(2)
    send_parts(1)
    send_home(2, 2, dqs.at[cell(2)])
    backward(3)
    send_parts(3)
    send_parts(2)
    send_home(2, 3, dqs.at[cell(3)])

    s_l = wsum[:, y, :, :, 0:128].astype(F32)
    s_r = wsum[:, :, x, :, 128:256].astype(F32)
    for e in range(1, 4):
        for c in stage1(e):
            c.wait_recv()
        s_l = s_l + wgot[0, e].astype(F32)
        s_r = s_r + wgot[1, e].astype(F32)
    w2[0] = s_l.astype(BF)
    w2[1] = s_r.astype(BF)
    for e in range(1, 4):
        for c in stage2(e):
            c.start()
    forward_parts(1)
    forward_parts(3)
    finish(0)

    s_l = w2[0, :, x].astype(F32)
    s_r = w2[1, :, y].astype(F32)
    for e in range(1, 4):
        for c in stage2(e):
            c.wait_recv()
        s_l = s_l + w2got[0, e].astype(F32)
        s_r = s_r + w2got[1, e].astype(F32)
    w3[:, :, 0:128] = s_l.astype(BF)
    w3[:, :, 128:256] = s_r.astype(BF)
    for e in range(1, 16):
        stage3(e).start()
    own_x = pltpu.make_async_copy(w3.at[zh], w3got.at[zh, :, cols(me)], loc.at[7])
    own_x.start()
    forward_parts(2)
    finish(1)
    finish(3)
    finish(2)
    own_x.wait()
    for e in range(1, 16):
        came = (at - e + 16) % 16
        spot = w3got.at[came // 4, :, cols(came % 4)]
        remote(spot, spot, x_s.at[e], x_r.at[e], sib, p).wait_recv()
    total = w3got[0].astype(F32)
    for i in range(1, 4):
        total = total + w3got[i].astype(F32)
    wo_ref[...] = total * (32768**-0.5)

    for kind in range(3):
        for o in range(1, 4):
            spot = (dk_hbm, dv_hbm, dq_hbm)[kind].at[:, cols((me - o + 4) % 4)]
            remote(spot, spot, f_s.at[kind, 0], f_r.at[kind, o], sib, p).wait_recv()
    for ll in range(4):
        sent_home(0, ll, fin.at[0, ll])
        sent_home(1, ll, fin.at[1, ll])
        sent_home(2, ll, dqs.at[cell(ll)])
    for kind in (K_, V_, Q_, C_):
        for i in range(3):
            spread(kind, i).wait_send()
    spread(G_, 0).wait_send()
    spread(G_, 1).wait_send()
    g_fwd.wait_send()
    for e in range(1, 4):
        for c in stage1(e) + stage2(e):
            c.wait_send()
    for e in range(1, 16):
        stage3(e).wait_send()
    for d in (UP, DOWN):

        def sent(d=d):
            for ll in range(4):
                for kind in (0, 1):
                    halo(d, ll, kind).wait_send()
                    part(d, ll, kind).wait_send()

        pl.when(has[d])(sent)
        for pos, ll in enumerate((mine, other, 2, 3)):
            for kind in (0, 1):
                r = WAY[pos, kind]
                if r:
                    pl.when(relays[d, r])(
                        lambda d=d: halo_forward(d, ll, kind, r).wait_send()
                    )
                r = WAY[pos, kind]
                if r:
                    pl.when(relays[d, r])(
                        lambda d=d: part_forward(d, pos, kind, r).wait_send()
                    )


def shards(queries, keys, values, out_grad, out_weight, pair_counts, counts):
    n, width = queries.shape
    big = pl.BlockSpec(memory_space=pltpu.HBM)
    dma = pltpu.SemaphoreType.DMA
    wide = jax.ShapeDtypeStruct((n, width), BF)
    return pl.pallas_call(
        kernel,
        name="cell_attention_backward",
        out_shape=(wide, wide, wide, jax.ShapeDtypeStruct((16, width), F32)),
        in_specs=[big] * 7,
        out_specs=(big, big, big, pl.BlockSpec(memory_space=pltpu.VMEM)),
        scratch_shapes=[
            pltpu.VMEM((2, 1536, GW), BF),
            pltpu.VMEM((2, GW, 1536), BF),
            pltpu.VMEM((512, GW), BF),
            pltpu.VMEM((512, 1024), BF),
            pltpu.VMEM((CELL, 1024), BF),
            pltpu.VMEM((CELL, 1024), BF),
            pltpu.VMEM((1024, GW), BF),
            pltpu.VMEM((512, GW), BF),
            pltpu.VMEM((4, 8, 128), jnp.int32),
            pltpu.VMEM((2, 8, 128), jnp.int32),
            pltpu.VMEM((1152, 256), F32),
            pltpu.VMEM((2, 3840, 256), BF),
            pltpu.VMEM((1152, 256), BF),
            pltpu.VMEM((4, 2, 8, 256), F32),
            pltpu.VMEM((GW, 512), BF),
            pltpu.VMEM((2, 1536, GW), F32),
            pltpu.VMEM((512, GW), BF),
            pltpu.VMEM((2, 4, CELL, GW), BF),
            pltpu.VMEM((2, 4, 2, CELL, GW), BF),
            pltpu.VMEM((2, 4, 2, CELL, GW), BF),
            pltpu.VMEM((2, 4, CELL, GW), BF),
            pltpu.VMEM((2, 4, CELL, GW), BF),
            pltpu.VMEM((4, 4, 4, 16, GW), BF),
            pltpu.VMEM((2, 4, 4, 4, 16, 128), BF),
            pltpu.VMEM((2, 4, 4, 16, 128), BF),
            pltpu.VMEM((2, 4, 4, 16, 128), BF),
            pltpu.VMEM((4, 16, GW), BF),
            pltpu.VMEM((4, 16, 1024), BF),
            pltpu.SMEM((1, 9), jnp.int32),
            pltpu.SMEM((1,), jnp.int32),
            dma((8,)),
            dma((5, 4)),
            dma((5, 4)),
            dma((2, 4, 2)),
            dma((2, 4, 2)),
            dma((2, 4)),
            dma((2, 4)),
            dma((2, 4, 2)),
            dma((2, 4, 2)),
            dma((2, 4)),
            dma((2, 4)),
            dma((3, 4)),
            dma((3, 4)),
            dma((2, 4)),
            dma((2, 4)),
            dma((16,)),
            dma((16,)),
            dma((2, 4)),
            dma((2, 4)),
        ],
        compiler_params=pltpu.CompilerParams(
            collective_id=0, has_side_effects=True, vmem_limit_bytes=53 * 2**20
        ),
        cost_estimate=pl.CostEstimate(
            flops=3_000_000_000, bytes_accessed=4_000_000, transcendentals=2_000_000
        ),
    )(queries, keys, values, out_grad, out_weight, pair_counts, counts)


def solution(mesh):
    both = P(("dz", "dxy"), None)
    return jax.shard_map(
        shards,
        mesh=mesh,
        in_specs=(both, both, both, both, P(), both, P(("dz", "dxy"))),
        out_specs=(both, both, both, P("dxy", None)),
        check_vma=False,
    )
```

```python
import jax
import jax.numpy as jnp
from jax import lax
from jax.experimental import pallas as pl
from jax.experimental.pallas import tpu as pltpu
from jax.sharding import PartitionSpec as P

MESH = pl.DeviceIdType.MESH
BF = jnp.bfloat16
F32 = jnp.float32
CELL = 128
GW = 256
DOWN, UP = 0, 1
K_, V_, Q_, G_, C_ = 0, 1, 2, 3, 4
WAY = {(0, 0): 1, (0, 1): 2, (1, 0): 3, (1, 1): 0, (2, 0): 1, (2, 1): 2, (3, 0): 3, (3, 1): 0}
VIA = {1: -15, 2: -3, 3: -12}
ONTO = {1: 16, 2: 4, 3: 13}
NEG = -1e30


def dot(a, b):
    return jnp.dot(a, b, preferred_element_type=F32)


def halves_t(x):
    row = lax.broadcasted_iota(jnp.int32, x.shape, 0)
    zero = jnp.zeros_like(x)
    return jnp.concatenate(
        [jnp.where(row < 64, x, zero), jnp.where(row < 64, zero, x)], axis=1
    )


def halves(x):
    lane = lax.broadcasted_iota(jnp.int32, x.shape, 1)
    zero = jnp.zeros_like(x)
    return jnp.concatenate(
        [jnp.where(lane < 64, x, zero), jnp.where(lane < 64, zero, x)], axis=0
    )


def diagonal(x):
    return jnp.concatenate([x[:64, :128], x[64:, 128:]], axis=0)


def kernel(
    q_hbm, k_hbm, v_hbm, g_hbm, w_hbm, pair_hbm, count_hbm,
    dq_hbm, dk_hbm, dv_hbm, wo_ref,
    kv, kvt, qs, gm, graw, gown, ww, do, pc, pcs,
    sbuf, pbuf, dsb, scale, att, acc, dqs,
    hold, back, got, hold2, fin, wsum, wgot, w2, w2got, w3, w3got,
    pair_ref, count_ref, loc, a_s, a_r, b_s, b_r, l_s, l_r, d_s, d_r, m_s, m_r, f_s, f_r, u_s, u_r, x_s, x_r, y_s, y_r,
):
    me = lax.axis_index("dz")
    p = lax.axis_index("dxy")
    low = me < 2
    sib = me + 1 - 2 * (me % 2)
    zpeer = (me + 2) % 4
    zdiag = (sib + 2) % 4
    group = (sib, zpeer, zdiag)
    places = 64

    def logical(layer, at):
        return jnp.where(at < 2, layer, 3 - layer)

    def layer_of(ll):
        return jnp.where(low, ll, 3 - ll)

    mine = logical(me, me)

    has = {DOWN: p > 0, UP: p < places - 1}
    gets = {DOWN: p < places - 1, UP: p > 0}
    step = {DOWN: -1, UP: 1}
    cross = {
        DOWN: (p % 16 == 0) & (p > 0),
        UP: (p % 16 == 15) & (p < places - 1),
    }
    crossed = {DOWN: (p % 16 == 15) & (p < places - 1), UP: (p % 16 == 0) & (p > 0)}
    relays = {}
    for r in (1, 2, 3):
        relays[UP, r] = (p % 16 == (15 + VIA[r]) % 16) & (p - VIA[r] < places - 1)
        relays[DOWN, r] = (p % 16 == -VIA[r] % 16) & (p + VIA[r] > 0)

    def via(d, r):
        return cl(p + step[d] * VIA[r])

    def relay_from(d, r):
        return cl(p - step[d] * VIA[r])

    def relay_to(d, r):
        return cl(p + step[d] * ONTO[r])

    def crossed_via(d, r):
        return cl(p - step[d] * ONTO[r])

    side = {DOWN: 2, UP: 0}

    def cl(x):
        return jnp.clip(x, 0, places - 1)

    def rows(ll, j):
        return pl.ds(pl.multiple_of((ll * 3 + j) * CELL, CELL), CELL)

    def cols(t):
        return pl.ds(pl.multiple_of(t * GW, GW), GW)

    def cell(ll):
        return pl.ds(pl.multiple_of(ll * CELL, CELL), CELL)

    def remote(src, dst, ss, rs, dz, place):
        return pltpu.make_async_remote_copy(
            src_ref=src, dst_ref=dst, send_sem=ss, recv_sem=rs,
            device_id=(dz, place), device_id_type=MESH,
        )

    own = cols(me)
    loads = [
        pltpu.make_async_copy(k_hbm.at[:, own], kv.at[0, rows(mine, 1)], loc.at[0]),
        pltpu.make_async_copy(v_hbm.at[:, own], kv.at[1, rows(mine, 1)], loc.at[1]),
        pltpu.make_async_copy(q_hbm.at[:, own], qs.at[cell(mine)], loc.at[2]),
        pltpu.make_async_copy(g_hbm, graw, loc.at[3]),
        pltpu.make_async_copy(w_hbm.at[:, own], ww, loc.at[4]),
    ]
    tables = [
        pltpu.make_async_copy(pair_hbm, pair_ref, loc.at[5]),
        pltpu.make_async_copy(count_hbm, count_ref, loc.at[6]),
    ]
    for c in tables + loads:
        c.start()

    zh, y, x = p // 16, (p // 4) % 4, p % 4
    at = zh * 4 + me

    def in_column(e):
        return zh * 16 + ((y + e) % 4) * 4 + x

    def in_row(e):
        return zh * 16 + y * 4 + (x + e) % 4

    def across(e):
        to = (at + e) % 16
        return to % 4, (to // 4) * 16 + y * 4 + x

    peers = []
    for e in range(1, 4):
        peers.append((None, me, in_column(e)))
        peers.append((None, me, in_row(e)))
    for e in range(1, 16):
        peers.append((None, *across(e)))
    for d in (DOWN, UP):
        peers.append((has[d], me, cl(p + step[d])))
        for r in (1, 2, 3):
            peers.append((cross[d], me, via(d, r)))
            peers.append((relays[d, r], me, relay_from(d, r)))
            peers.append((relays[d, r], me, relay_to(d, r)))
            peers.append((crossed[d], me, crossed_via(d, r)))
    barrier = pltpu.get_barrier_semaphore()
    expect = 0
    for ok, a, b in peers:

        def greet(a=a, b=b):
            pl.semaphore_signal(barrier, inc=1, device_id=(a, b), device_id_type=MESH)

        if ok is None:
            greet()
            expect = expect + 1
        else:
            pl.when(ok)(greet)
            expect = expect + jnp.where(ok, 1, 0)

    for c in tables:
        c.wait()
    lane = lax.broadcasted_iota(jnp.int32, (8, 128), 1)
    plain = jnp.zeros((8, 128), jnp.int32)
    turned = jnp.zeros((8, 128), jnp.int32)
    for s in range(9):
        plain = jnp.where(lane == s, pair_ref[0, s], plain)
        turned = jnp.where(lane == (2 - s // 3) * 3 + s % 3, pair_ref[0, s], turned)
    pcs[0] = plain
    pcs[1] = turned
    pc[mine] = jnp.where(low, plain, turned)

    def clear(d):
        for ll in range(4):
            kv[:, (ll * 3 + side[d]) * CELL : (ll * 3 + side[d] + 1) * CELL, :] = (
                jnp.zeros((2, CELL, GW), BF)
            )
            got[d, ll] = jnp.zeros((2, CELL, GW), BF)

    for d in (DOWN, UP):
        pl.when(jnp.logical_not(gets[d]))(lambda d=d: clear(d))

    pl.semaphore_wait(barrier, expect)

    def landing(kind, ll):
        if kind == C_:
            return pc.at[ll]
        if kind in (K_, V_):
            return kv.at[kind, rows(ll, 1)]
        return {Q_: qs, G_: gm}[kind].at[cell(ll)]

    def spread(kind, i):
        t = group[i]
        lt = logical(me, t)
        if kind == C_:
            src = pcs.at[jnp.where(t < 2, 0, 1)]
        elif kind == G_:
            src = gown
        else:
            src = {K_: k_hbm, V_: v_hbm, Q_: q_hbm}[kind].at[:, cols(t)]
        return remote(
            src, landing(kind, lt), a_s.at[kind, i], a_r.at[kind, lt], t, p
        )

    def arrived(kind, ll):
        dst = landing(kind, ll)
        remote(dst, dst, a_s.at[kind, 0], a_r.at[kind, ll], sib, p).wait_recv()

    for kind in (K_, V_, C_):
        for i in range(3):
            spread(kind, i).start()
    spread(Q_, 0).start()

    def halo(d, ll, kind):
        blk = kv.at[kind, rows(ll, 1)]
        dst = kv.at[kind, rows(ll, side[d])]
        return remote(
            blk, dst, b_s.at[d, ll, kind], b_r.at[d, ll, kind], me, cl(p + step[d])
        )

    def halo_detour(d, ll, kind, r):
        blk = kv.at[kind, rows(ll, 1)]
        return remote(
            blk, hold.at[d, ll], b_s.at[d, ll, kind], l_r.at[d, ll], me, via(d, r)
        )

    def halo_forward(d, ll, kind, r):
        dst = kv.at[kind, rows(ll, side[d])]
        return remote(
            hold.at[d, ll], dst, l_s.at[d, ll], b_r.at[d, ll, kind], me, relay_to(d, r)
        )

    def part(d, ll, kind):
        return remote(
            back.at[d, ll, kind], got.at[d, ll, kind],
            d_s.at[d, ll, kind], d_r.at[d, ll, kind], me, cl(p + step[d]),
        )

    def part_detour(d, ll, kind, r):
        return remote(
            back.at[d, ll, kind], hold2.at[d, ll],
            d_s.at[d, ll, kind], m_r.at[d, ll], me, via(d, r),
        )

    def part_forward(d, ll, kind, r):
        return remote(
            hold2.at[d, ll], got.at[d, ll, kind],
            m_s.at[d, ll], d_r.at[d, ll, kind], me, relay_to(d, r),
        )

    def send_beside(pos, ll, kind, straight, detour):
        r = WAY[pos, kind]
        for d in (UP, DOWN):
            if r == 0:
                pl.when(has[d])(lambda d=d: straight(d, ll, kind).start())
            else:
                pl.when(has[d] & jnp.logical_not(cross[d]))(
                    lambda d=d: straight(d, ll, kind).start()
                )
                pl.when(cross[d])(lambda d=d: detour(d, ll, kind, r).start())

    def pass_on(pos, ll, detour, forward):
        for kind in (0, 1):
            r = WAY[pos, kind]
            if r == 0:
                continue
            for d in (UP, DOWN):

                def go(d=d):
                    detour(d, ll, kind, r).wait_recv()
                    forward(d, ll, kind, r).start()

                pl.when(relays[d, r])(go)

    def send_halo(pos, ll, kind):
        send_beside(pos, ll, kind, halo, halo_detour)

    def forward_halo(pos, ll):
        pass_on(pos, ll, halo_detour, halo_forward)

    other = 1 - mine
    loads[0].wait()
    send_halo(0, mine, 0)
    loads[1].wait()
    send_halo(0, mine, 1)
    loads[3].wait()
    live = lax.broadcasted_iota(jnp.int32, (CELL, 1024), 0) < count_ref[0]
    gown[...] = jnp.where(live, graw[...], jnp.zeros((CELL, 1024), BF))
    own_g = pltpu.make_async_copy(gown, gm.at[cell(mine)], loc.at[5])
    own_g.start()
    spread(G_, 0).start()
    for kind in (0, 1):
        arrived(kind, other)
        send_halo(1, other, kind)
    forward_halo(0, mine)
    for kind in (0, 1):
        for ll in (2, 3):
            arrived(kind, ll)
            send_halo(ll, ll, kind)
        if kind == 0:
            spread(Q_, 1).start()
            spread(Q_, 2).start()
            forward_halo(1, other)
    spread(G_, 1).start()
    zl = logical(zpeer, me)
    g_fwd = remote(
        gm.at[cell(zl)], gm.at[cell(zl)], a_s.at[G_, 2], a_r.at[G_, zl], sib, p
    )

    def halo_arrived(ll):
        for d in (UP, DOWN):
            for kind in (0, 1):
                pl.when(gets[d])(lambda d=d, kind=kind: halo(d, ll, kind).wait_recv())

    def turn_layer(ll):
        for j in range(3):
            for kind in (0, 1):
                at_ = (ll * 3 + j) * CELL
                kvt[kind, :, at_ : at_ + CELL] = kv[kind, at_ : at_ + CELL, :].T

    first = [0, 0, 1, 2]
    last = [1, 2, 3, 3]
    base = [0, 768, 1920, 3072]
    sub = lax.broadcasted_iota(jnp.int32, (CELL, 128), 0)

    def fold(op, v):
        return op(v.reshape(CELL // 8, 8, 256), axis=0)

    def forward(lq):
        bias = jnp.where(sub < pc[lq][0:1, :], 0.0, NEG)
        slots = [(ll, j) for ll in range(first[lq], last[lq] + 1) for j in range(3)]
        n = len(slots) * CELL
        r0 = first[lq] * 3 * CELL
        cq = slice(lq * CELL, (lq + 1) * CELL)
        for hp in range(2):
            hc = slice(hp * 128, hp * 128 + 128)
            qt = halves_t((qs[cq, hc] * jnp.asarray(0.125, BF)).T)
            top = None
            for i, (ll, j) in enumerate(slots):
                at_ = (ll * 3 + j) * CELL
                k9 = (ll - lq + 1) * 3 + j
                s = dot(kv[0, at_ : at_ + CELL, hc], qt) + bias[:, k9 : k9 + 1]
                sbuf[i * CELL : (i + 1) * CELL, :] = s
                t = fold(jnp.max, s)
                top = t if top is None else jnp.maximum(top, t)
            top = jnp.max(top, axis=0, keepdims=True)
            total = None
            b0 = base[lq]
            for i in range(len(slots)):
                e = jnp.exp(sbuf[i * CELL : (i + 1) * CELL, :] - top)
                pbuf[hp, b0 + i * CELL : b0 + (i + 1) * CELL, :] = e.astype(BF)
                t = fold(jnp.sum, e)
                total = t if total is None else total + t
            inv = 1.0 / jnp.sum(total, axis=0, keepdims=True)
            at_t = dot(kvt[1, hc, r0 : r0 + n], pbuf[hp, b0 : b0 + n, :])
            att[hc, cq] = diagonal(at_t * inv).astype(BF)
            scale[lq, hp] = jnp.broadcast_to(inv, (8, 256))

    def backward(lq):
        slots = [(ll, j) for ll in range(first[lq], last[lq] + 1) for j in range(3)]
        n = len(slots) * CELL
        r0 = first[lq] * 3 * CELL
        cq = slice(lq * CELL, (lq + 1) * CELL)
        b0 = base[lq]
        for hp in range(2):
            hc = slice(hp * 128, hp * 128 + 128)
            inv = scale[lq, hp][0:1, :]
            inv = jnp.concatenate(
                [
                    jnp.broadcast_to(inv[:, :128], (64, 128)),
                    jnp.broadcast_to(inv[:, 128:], (64, 128)),
                ],
                axis=0,
            )
            dt = (do[cq, hc].T.astype(F32) * inv).astype(BF)
            prod = dt.astype(F32) * att[hc, cq].astype(F32)
            dl = jnp.concatenate(
                [
                    jnp.sum(prod[:64], axis=0, keepdims=True),
                    jnp.sum(prod[64:], axis=0, keepdims=True),
                ],
                axis=1,
            )
            dmt = halves_t(dt)
            dm = halves(dt.T)
            qm = halves(qs[cq, hc] * jnp.asarray(0.125, BF))
            for i, (ll, j) in enumerate(slots):
                at_ = (ll * 3 + j) * CELL
                pr = pbuf[hp, b0 + i * CELL : b0 + (i + 1) * CELL, :]
                dp = dot(kv[1, at_ : at_ + CELL, hc], dmt)
                ds = (pr.astype(F32) * (dp - dl)).astype(BF)
                dsb[i * CELL : (i + 1) * CELL, :] = ds
                dv = dot(pr, dm)
                dk = dot(ds, qm)
                if lq == max(ll - 1, 0):
                    acc[1, at_ : at_ + CELL, hc] = dv
                    acc[0, at_ : at_ + CELL, hc] = dk
                else:
                    acc[1, at_ : at_ + CELL, hc] += dv
                    acc[0, at_ : at_ + CELL, hc] += dk
            dqt = dot(kvt[0, hc, r0 : r0 + n], dsb[0:n, :])
            dqs[cq, hc] = (diagonal(dqt) * 0.125).T.astype(BF)

    def send_parts(ll):
        for d in (UP, DOWN):
            j = 2 if d == UP else 0
            at_ = (ll * 3 + j) * CELL
            for kind in (1, 0):
                back[d, ll, kind] = acc[kind, at_ : at_ + CELL, :].astype(BF)
        for kind in (1, 0):
            send_beside(ll, ll, kind, part, part_detour)

    def forward_parts(ll):
        pass_on(ll, ll, part_detour, part_forward)

    def home(kind, ll, src):
        t = layer_of(ll)
        out = (dk_hbm, dv_hbm, dq_hbm)[kind].at[:, cols(me)]
        o = (t - me + 4) % 4
        return remote(src, out, f_s.at[kind, ll], f_r.at[kind, o], t, p)

    def keep(kind, ll, src):
        out = (dk_hbm, dv_hbm, dq_hbm)[kind].at[:, cols(me)]
        return pltpu.make_async_copy(src, out, f_s.at[kind, ll])

    def send_home(kind, ll, src):
        if ll >= 2:
            home(kind, ll, src).start()
        else:
            pl.when(mine != ll)(lambda: home(kind, ll, src).start())
            pl.when(mine == ll)(lambda: keep(kind, ll, src).start())

    def sent_home(kind, ll, src):
        if ll >= 2:
            home(kind, ll, src).wait_send()
        else:
            pl.when(mine != ll)(lambda: home(kind, ll, src).wait_send())
            pl.when(mine == ll)(lambda: keep(kind, ll, src).wait())

    def finish(ll):
        for d in (UP, DOWN):
            for kind in (0, 1):
                pl.when(gets[d])(lambda d=d, kind=kind: part(d, ll, kind).wait_recv())
        at_ = (ll * 3 + 1) * CELL
        for kind in (0, 1):
            s = acc[kind, at_ : at_ + CELL, :]
            s = s + got[0, ll, kind].astype(F32) + got[1, ll, kind].astype(F32)
            fin[kind, ll] = s.astype(BF)
            send_home(kind, ll, fin.at[kind, ll])

    left, right = pl.ds(0, 128), pl.ds(128, 128)

    def stage1(e):
        return (
            remote(
                wsum.at[:, (y + e) % 4, :, :, left], wgot.at[0, e],
                u_s.at[0, e], u_r.at[0, e], me, in_column(e),
            ),
            remote(
                wsum.at[:, :, (x + e) % 4, :, right], wgot.at[1, e],
                u_s.at[1, e], u_r.at[1, e], me, in_row(e),
            ),
        )

    def stage2(e):
        return (
            remote(
                w2.at[0, :, (x + e) % 4], w2got.at[0, e],
                y_s.at[0, e], y_r.at[0, e], me, in_row(e),
            ),
            remote(
                w2.at[1, :, (y + e) % 4], w2got.at[1, e],
                y_s.at[1, e], y_r.at[1, e], me, in_column(e),
            ),
        )

    def stage3(e):
        t, place = across(e)
        to = (at + e) % 16
        return remote(
            w3.at[to // 4], w3got.at[zh, :, cols(me)], x_s.at[e], x_r.at[e], t, place
        )

    loads[2].wait()
    loads[4].wait()
    own_g.wait()
    for kind in (C_, Q_, G_):
        arrived(kind, other)
    do[0 : 2 * CELL] = dot(gm[0 : 2 * CELL], ww[...]).astype(BF)
    forward_halo(3, 3)
    forward_halo(2, 2)
    halo_arrived(0)
    turn_layer(0)
    halo_arrived(1)
    turn_layer(1)
    forward(0)
    backward(0)
    send_home(2, 0, dqs.at[cell(0)])
    halo_arrived(2)
    turn_layer(2)
    forward(1)
    backward(1)
    send_parts(0)
    send_home(2, 1, dqs.at[cell(1)])
    for kind in (C_, Q_):
        arrived(kind, 2)
        arrived(kind, 3)
    halo_arrived(3)
    turn_layer(3)
    forward(2)
    arrived(G_, zl)
    g_fwd.start()
    forward(3)
    forward_parts(0)
    arrived(G_, 5 - zl)
    for i in range(4):
        w_t = dot(att[...], gm[:, i * 256 : (i + 1) * 256]).astype(BF)
        wsum[i] = w_t.T.reshape(4, 4, 16, GW)
    for e in range(1, 4):
        for c in stage1(e):
            c.start()
    do[2 * CELL : 4 * CELL] = dot(gm[2 * CELL : 4 * CELL], ww[...]).astype(BF)
    backward(2)
    send_parts(1)
    send_home(2, 2, dqs.at[cell(2)])
    backward(3)
    send_parts(3)
    send_parts(2)
    send_home(2, 3, dqs.at[cell(3)])

    s_l = wsum[:, y, :, :, 0:128].astype(F32)
    s_r = wsum[:, :, x, :, 128:256].astype(F32)
    for e in range(1, 4):
        for c in stage1(e):
            c.wait_recv()
        s_l = s_l + wgot[0, e].astype(F32)
        s_r = s_r + wgot[1, e].astype(F32)
    w2[0] = s_l.astype(BF)
    w2[1] = s_r.astype(BF)
    for e in range(1, 4):
        for c in stage2(e):
            c.start()
    forward_parts(1)
    forward_parts(3)
    finish(0)

    s_l = w2[0, :, x].astype(F32)
    s_r = w2[1, :, y].astype(F32)
    for e in range(1, 4):
        for c in stage2(e):
            c.wait_recv()
        s_l = s_l + w2got[0, e].astype(F32)
        s_r = s_r + w2got[1, e].astype(F32)
    w3[:, :, 0:128] = s_l.astype(BF)
    w3[:, :, 128:256] = s_r.astype(BF)
    for e in range(1, 16):
        stage3(e).start()
    own_x = pltpu.make_async_copy(w3.at[zh], w3got.at[zh, :, cols(me)], loc.at[7])
    own_x.start()
    forward_parts(2)
    finish(1)
    finish(3)
    finish(2)
    own_x.wait()
    for e in range(1, 16):
        came = (at - e + 16) % 16
        spot = w3got.at[came // 4, :, cols(came % 4)]
        remote(spot, spot, x_s.at[e], x_r.at[e], sib, p).wait_recv()
    total = w3got[0].astype(F32)
    for i in range(1, 4):
        total = total + w3got[i].astype(F32)
    wo_ref[...] = total * (32768**-0.5)

    for kind in range(3):
        for o in range(1, 4):
            spot = (dk_hbm, dv_hbm, dq_hbm)[kind].at[:, cols((me - o + 4) % 4)]
            remote(spot, spot, f_s.at[kind, 0], f_r.at[kind, o], sib, p).wait_recv()
    for ll in range(4):
        sent_home(0, ll, fin.at[0, ll])
        sent_home(1, ll, fin.at[1, ll])
        sent_home(2, ll, dqs.at[cell(ll)])
    for kind in (K_, V_, Q_, C_):
        for i in range(3):
            spread(kind, i).wait_send()
    spread(G_, 0).wait_send()
    spread(G_, 1).wait_send()
    g_fwd.wait_send()
    for e in range(1, 4):
        for c in stage1(e) + stage2(e):
            c.wait_send()
    for e in range(1, 16):
        stage3(e).wait_send()
    for d in (UP, DOWN):

        def sent(d=d):
            for ll in range(4):
                for kind in (0, 1):
                    halo(d, ll, kind).wait_send()
                    part(d, ll, kind).wait_send()

        pl.when(has[d])(sent)
        for pos, ll in enumerate((mine, other, 2, 3)):
            for kind in (0, 1):
                r = WAY[pos, kind]
                if r:
                    pl.when(relays[d, r])(
                        lambda d=d: halo_forward(d, ll, kind, r).wait_send()
                    )
                r = WAY[pos, kind]
                if r:
                    pl.when(relays[d, r])(
                        lambda d=d: part_forward(d, pos, kind, r).wait_send()
                    )


def shards(queries, keys, values, out_grad, out_weight, pair_counts, counts):
    n, width = queries.shape
    big = pl.BlockSpec(memory_space=pltpu.HBM)
    dma = pltpu.SemaphoreType.DMA
    wide = jax.ShapeDtypeStruct((n, width), BF)
    return pl.pallas_call(
        kernel,
        name="cell_attention_backward",
        out_shape=(wide, wide, wide, jax.ShapeDtypeStruct((16, width), F32)),
        in_specs=[big] * 7,
        out_specs=(big, big, big, pl.BlockSpec(memory_space=pltpu.VMEM)),
        scratch_shapes=[
            pltpu.VMEM((2, 1536, GW), BF),
            pltpu.VMEM((2, GW, 1536), BF),
            pltpu.VMEM((512, GW), BF),
            pltpu.VMEM((512, 1024), BF),
            pltpu.VMEM((CELL, 1024), BF),
            pltpu.VMEM((CELL, 1024), BF),
            pltpu.VMEM((1024, GW), BF),
            pltpu.VMEM((512, GW), BF),
            pltpu.VMEM((4, 8, 128), jnp.int32),
            pltpu.VMEM((2, 8, 128), jnp.int32),
            pltpu.VMEM((1152, 256), F32),
            pltpu.VMEM((2, 3840, 256), BF),
            pltpu.VMEM((1152, 256), BF),
            pltpu.VMEM((4, 2, 8, 256), F32),
            pltpu.VMEM((GW, 512), BF),
            pltpu.VMEM((2, 1536, GW), F32),
            pltpu.VMEM((512, GW), BF),
            pltpu.VMEM((2, 4, CELL, GW), BF),
            pltpu.VMEM((2, 4, 2, CELL, GW), BF),
            pltpu.VMEM((2, 4, 2, CELL, GW), BF),
            pltpu.VMEM((2, 4, CELL, GW), BF),
            pltpu.VMEM((2, 4, CELL, GW), BF),
            pltpu.VMEM((4, 4, 4, 16, GW), BF),
            pltpu.VMEM((2, 4, 4, 4, 16, 128), BF),
            pltpu.VMEM((2, 4, 4, 16, 128), BF),
            pltpu.VMEM((2, 4, 4, 16, 128), BF),
            pltpu.VMEM((4, 16, GW), BF),
            pltpu.VMEM((4, 16, 1024), BF),
            pltpu.SMEM((1, 9), jnp.int32),
            pltpu.SMEM((1,), jnp.int32),
            dma((8,)),
            dma((5, 4)),
            dma((5, 4)),
            dma((2, 4, 2)),
            dma((2, 4, 2)),
            dma((2, 4)),
            dma((2, 4)),
            dma((2, 4, 2)),
            dma((2, 4, 2)),
            dma((2, 4)),
            dma((2, 4)),
            dma((3, 4)),
            dma((3, 4)),
            dma((2, 4)),
            dma((2, 4)),
            dma((16,)),
            dma((16,)),
            dma((2, 4)),
            dma((2, 4)),
        ],
        compiler_params=pltpu.CompilerParams(
            collective_id=0, has_side_effects=True, vmem_limit_bytes=53 * 2**20
        ),
        cost_estimate=pl.CostEstimate(
            flops=3_000_000_000, bytes_accessed=4_000_000, transcendentals=2_000_000
        ),
    )(queries, keys, values, out_grad, out_weight, pair_counts, counts)


def solution(mesh):
    both = P(("dz", "dxy"), None)
    return jax.shard_map(
        shards,
        mesh=mesh,
        in_specs=(both, both, both, both, P(), both, P(("dz", "dxy"))),
        out_specs=(both, both, both, P("dxy", None)),
        check_vma=False,
    )
```
